256 devices in a mesh: cell: 64 (over z, x, y_lo), lev: 4 (over y_hi, core).
Axes of the slice: x: 4, y: 4 (y_hi: 2, y_lo: 2; y = y_hi * 2 + y_lo), z: 8, core: 2. Of those that a mesh axis runs over, the one named last changes fastest.
Arguments:
- populations: float32 [4096, 8192], P('cell', 'lev'), may hold values from 0.5 to 1.5
- rate_blocks: bfloat16 [2, 64, 6, 128, 128], P(None, 'lev'), may hold values from -0.21875 to 0.21875
- pattern: int32 [64, 6], P('lev'), may hold values from 0 to 63, as said below
- bracket: int32 [4096], P('cell'), may hold values from 0 to 1
- cross_section: float32 [8192], P('lev'), as said below
- emission: float32 [8192], P('lev'), may hold values from 0.1 to 1
- absorber: float32 [4096], P('cell'), as said below
- stream_speed: float32 [4096], P('cell'), may hold values from 0.25 to 1
- cross_speed: float32 [4096], P('cell'), may hold values from -1 to 1
- inflow: float32 [16, 8192], P(None, 'lev'), may hold values from 0.5 to 1.5
Outputs:
- updated: float32 [4096, 8192], P('cell', 'lev')
- absorption: float32 [4096, 8192], P('cell', 'lev')
The draws below stay inside these ranges and needn't reach their ends.
Inputs may be any that keep to these rules, and one draw needn't show every extreme that they name: Row r of pattern lists 6 distinct level blocks, the first of them r itself. `cross_section`: each cross section lies between 0.1 / 256 and 0.035. `absorber`: absorber columns lie between 0.5 and 2, except a few whole streamwise rows where they equal 384.
All inputs are finite; a program needn't handle non-finite values.
Results may differ from the reference program's by a relative error of at most 0.00055.
Values may be sent and summed in bfloat16 or wider, within the bound.
No kernel may reach another device: no remote copies, remote signals or barrier semaphores. Data moves between devices by JAX's collectives and lax.ppermute only.
A program may use at most 128 MiB of HBM per device.

```python
import math
import jax
import jax.numpy as jnp
from jax import lax

LEVELS = 8192
BLOCK = 128
NZB = 6
NBR = 2
NY = 16
NBLOCKS = 64
STREAMWISE_NUM = 256
CELLS = 4096


def draw_pattern(key, part):
    block_count = LEVELS // BLOCK
    row_keys = jax.random.split(jax.random.fold_in(key, 3), block_count)

    def one_row(row_key, row_index):
        shuffled = jax.random.permutation(row_key, block_count - 1)[:NZB - 1]
        others = (row_index + 1 + shuffled) % block_count
        return jnp.concatenate([row_index[None], others]).astype(jnp.int32)
    return jax.vmap(one_row)(row_keys, jnp.arange(block_count, dtype=jnp.int32))


def draw_cross_section(key, part):
    key_pick, key_fast, key_slow = jax.random.split(jax.random.fold_in(key, 5), 3)
    fast_share = 0.5
    is_fast = jax.random.uniform(key_pick, (LEVELS,)) < fast_share
    fast_value = jnp.exp(jax.random.uniform(key_fast, (LEVELS,), minval=math.log(0.02), maxval=math.log(0.035)))
    slow_value = jnp.exp(jax.random.uniform(key_slow, (LEVELS,), minval=math.log(0.1), maxval=math.log(0.3))) / STREAMWISE_NUM
    return jnp.where(is_fast, fast_value, slow_value).astype(jnp.float32)


def draw_absorber(key, part):
    key_background, key_pulse = jax.random.split(jax.random.fold_in(key, 9))
    baseline_level = jnp.exp(jax.random.uniform(key_background, (STREAMWISE_NUM, NY), minval=math.log(0.5), maxval=math.log(2.0)))
    pulse_rows = jax.random.randint(key_pulse, (3,), 0, STREAMWISE_NUM)
    inside_pulse = jnp.any(jnp.arange(STREAMWISE_NUM)[:, None] == pulse_rows[None, :], axis=1)
    number_density = jnp.where(inside_pulse[:, None], 1.5 * STREAMWISE_NUM, baseline_level)
    return number_density.reshape(STREAMWISE_NUM * NY).astype(jnp.float32)


def place_ends(values, rng, least, high):
    extent = values.shape
    place = [jax.random.randint(jax.random.fold_in(rng, axis), (), 0, extent[axis]) for axis in range(len(extent))]
    values = values.at[tuple(place)].set(least)
    longest = extent.index(max(extent))
    place[longest] = (place[longest] + 1) % extent[longest]
    return values.at[tuple(place)].set(high)


def shard_levels(rng, dims, shards, least, largest):
    def one(dim, parts):
        steps = jax.random.uniform(jax.random.fold_in(jax.random.fold_in(rng, 6), dim), (parts,), jnp.float32, least / len(shards), largest / len(shards))
        return jnp.repeat(jnp.exp(steps), dims[dim] // parts).reshape((-1,) + (1,) * (len(dims) - dim - 1))

    factor_of = one(*shards[0])
    for cut in shards[1:]:
        factor_of = factor_of * one(*cut)
    return factor_of


def scatter_about(rng, dims, spread, limit, cuts=(), kind=jnp.bfloat16):
    result = jax.random.normal(rng, dims, jnp.float32) * spread
    if len(cuts) > 0:
        result = shard_levels(rng, dims, cuts, -0.22, 0.18) * result
    return jnp.clip(result, min=-limit, max=limit).astype(kind)


def setup_inputs(seed: int = 0) -> dict:
    key_of = jax.random.split(jax.random.key(seed), 11)
    populations = jnp.clip(0.5 + 1.0 * jax.random.uniform(key_of[0], (CELLS, LEVELS), jnp.float32) ** shard_levels(key_of[0], (CELLS, LEVELS), ((0, 64), (1, 4)), -0.2, 0.2), 0.5, 1.5)
    rate_blocks = scatter_about(key_of[1], (NBR, NBLOCKS, NZB, BLOCK, BLOCK), (NZB * BLOCK) ** -0.5, 0.21875, ((1, 4),))
    pattern = draw_pattern(jax.random.fold_in(key_of[10], 71), 0)
    bracket = place_ends(jax.random.randint(key_of[3], (CELLS,), 0, NBR), jax.random.fold_in(key_of[3], 1), 0, NBR - 1).astype(jnp.int32)
    cross_section = draw_cross_section(jax.random.fold_in(key_of[10], 71), 0)
    emission = jnp.clip(jnp.exp(math.log(1.0) - 2.3025851 * jax.random.uniform(key_of[5], (LEVELS,), jnp.float32) ** shard_levels(key_of[5], (LEVELS,), ((0, 4),), -0.2, 0.2)), 0.1, 1.0)
    absorber = draw_absorber(jax.random.fold_in(key_of[10], 71), 0)
    stream_speed = jnp.clip(0.25 + 0.75 * jax.random.uniform(key_of[7], (CELLS,), jnp.float32) ** shard_levels(key_of[7], (CELLS,), ((0, 64),), -0.2, 0.2), 0.25, 1.0)
    cross_speed = jnp.clip(jax.random.uniform(key_of[8], (CELLS,), jnp.float32, -1.0, 1.0) * shard_levels(key_of[8], (CELLS,), ((0, 64),), -0.4, 0.0), -1.0, 1.0)
    inflow = jnp.clip(0.5 + 1.0 * jax.random.uniform(key_of[9], (NY, LEVELS), jnp.float32) ** shard_levels(key_of[9], (NY, LEVELS), ((1, 4),), -0.2, 0.2), 0.5, 1.5)
    return {"populations": populations, "rate_blocks": rate_blocks, "pattern": pattern, "bracket": bracket, "cross_section": cross_section, "emission": emission, "absorber": absorber, "stream_speed": stream_speed, "cross_speed": cross_speed, "inflow": inflow}


time_step = 0.25


def rate_term(populations, rate_blocks, pattern, bracket):
    lowered = lax.optimization_barrier(populations.astype(jnp.bfloat16)).astype(jnp.float32)
    blocks_all = lowered.reshape(CELLS, NBLOCKS, BLOCK)

    def one_row(row_block):
        columns = blocks_all[:, pattern[row_block], :]
        summed = jnp.zeros((CELLS, BLOCK), jnp.float32)
        for bracket_id in range(NBR):
            table = rate_blocks[bracket_id, row_block].astype(jnp.float32)
            product = jnp.einsum("ckj,kij->ci", columns, table)
            summed = jnp.where((bracket == bracket_id)[:, None], product, summed)
        return summed

    stacked = lax.map(one_row, jnp.arange(NBLOCKS, dtype=jnp.int32))
    return jnp.transpose(stacked, (1, 0, 2)).reshape(CELLS, LEVELS)


def radiation(populations, emission, cross_section, absorber):
    emitted = populations * emission[None, :]
    transmit = jnp.exp(-(absorber[:, None] * cross_section[None, :]))
    layered_pass = transmit.reshape(STREAMWISE_NUM, NY, LEVELS)
    layered_emit = emitted.reshape(STREAMWISE_NUM, NY, LEVELS)

    def advance(running, layer_in):
        transmit_x, source_x = layer_in
        renewed = transmit_x * running + source_x
        return renewed, renewed

    nothing = jnp.zeros((NY, LEVELS), jnp.float32)
    _, downward = lax.scan(advance, nothing, (layered_pass, layered_emit))
    _, upward = lax.scan(advance, nothing, (layered_pass, layered_emit), reverse=True)
    absorbed = (1.0 - layered_pass) * (downward + upward - 2.0 * layered_emit)
    return emitted, absorbed.reshape(CELLS, LEVELS)


def advection(populations, inflow, stream_speed, cross_speed):
    layered = populations.reshape(STREAMWISE_NUM, NY, LEVELS)
    upstream = jnp.concatenate([inflow[None], layered[:-1]], axis=0)
    before_y = jnp.roll(layered, 1, axis=1)
    after_y = jnp.roll(layered, -1, axis=1)
    along_x = stream_speed.reshape(STREAMWISE_NUM, NY, 1)
    along_y = cross_speed.reshape(STREAMWISE_NUM, NY, 1)
    flux_sum = -along_x * (layered - upstream) - jnp.maximum(along_y, 0.0) * (layered - before_y) - jnp.minimum(along_y, 0.0) * (after_y - layered)
    return flux_sum.reshape(CELLS, LEVELS)


def tendency(populations, rate_blocks, pattern, bracket, cross_section, emission, absorber, stream_speed, cross_speed, inflow):
    rates_part = rate_term(populations, rate_blocks, pattern, bracket)
    emitted, absorbed = radiation(populations, emission, cross_section, absorber)
    carried = advection(populations, inflow, stream_speed, cross_speed)
    return rates_part - emitted + absorbed + carried, absorbed


def reference(populations, rate_blocks, pattern, bracket, cross_section, emission, absorber, stream_speed, cross_speed, inflow):
    first_rate, _ = tendency(populations, rate_blocks, pattern, bracket, cross_section, emission, absorber, stream_speed, cross_speed, inflow)
    middle = populations + time_step * first_rate
    second, absorption = tendency(middle, rate_blocks, pattern, bracket, cross_section, emission, absorber, stream_speed, cross_speed, inflow)
    updated = 0.5 * (populations + middle + time_step * second)
    return (updated, absorption)
```

```python
import functools

import jax
import jax.numpy as jnp
from jax import lax
from jax.experimental import pallas as pl
from jax.experimental.pallas import tpu as pltpu
from jax.sharding import PartitionSpec as P

NY = 16
LANES = 128
ROWS = 8
time_step = 0.25


def column(row):
    n = row.shape[1]
    at_row = lax.broadcasted_iota(jnp.int32, (n, n), 0)
    at_column = lax.broadcasted_iota(jnp.int32, (n, n), 1)
    return jnp.sum(jnp.where(at_row == at_column, row, jnp.zeros_like(row)), axis=1, keepdims=True)


def layers(value):
    return [value[k : k + NY] for k in range(0, value.shape[0], NY)]


def exits(passed, emitted):
    down, up = emitted[0], emitted[-1]
    for t, e in zip(passed[1:], emitted[1:]):
        down = t * down + e
    for t, e in zip(passed[-2::-1], emitted[-2::-1]):
        up = t * up + e
    return down, up


def put_exits(exit_ref, group, groups, down, up):
    for way, value in enumerate((down, up)):
        for half in range(NY // ROWS):
            at = (way * (NY // ROWS) + half) * groups + group
            exit_ref[at] = value[half * ROWS : (half + 1) * ROWS]


def get_enters(enter_ref, group, groups):
    found = []
    for way in range(2):
        halves = [enter_ref[(way * (NY // ROWS) + half) * groups + group] for half in range(NY // ROWS)]
        found.append(jnp.concatenate(halves, axis=0))
    return found


def absorbed_of(passed, emitted, enter_down, enter_up):
    count = len(passed)
    downward, upward = [None] * count, [None] * count
    running = enter_down
    for k in range(count):
        running = passed[k] * running + emitted[k]
        downward[k] = running
    running = enter_up
    for k in reversed(range(count)):
        running = passed[k] * running + emitted[k]
        upward[k] = running
    return [
        (1.0 - t) * (d + u - 2.0 * e) for t, d, u, e in zip(passed, downward, upward, emitted)
    ]


def advection(layered, boundary, along_x, forward_y, backward_y):
    result, upstream = [], boundary
    for k, here in enumerate(layered):
        before = pltpu.roll(here, 1, 0)
        after = pltpu.roll(here, NY - 1, 0)
        result.append(
            -along_x[k] * (here - upstream) - forward_y[k] * (here - before) - backward_y[k] * (after - here)
        )
        upstream = here
    return result


def first_kernel(p_ref, cross_ref, emission_ref, absorber_ref, q_ref, last_ref, exit_ref):
    absorber = column(absorber_ref[...])
    groups = p_ref.shape[1] // LANES
    for g in range(groups):
        at = slice(g * LANES, (g + 1) * LANES)
        p = p_ref[:, at]
        q = p.astype(jnp.bfloat16)
        q_ref[:, at] = q
        last_ref[:, at] = q[-NY:]
        passed = layers(jnp.exp(-(absorber * cross_ref[:, at])))
        emitted = layers(p * emission_ref[:, at])
        put_exits(exit_ref, g, groups, *exits(passed, emitted))


def scan(exit_ref, pass_ref, enter_ref, way):
    count = exit_ref.shape[0]

    def step(i, carry):
        at = jnp.where(way == 0, i, count - 1 - i)
        enter_ref[at] = carry
        return pass_ref[at] * carry + exit_ref[at]

    lax.fori_loop(0, count, step, jnp.zeros(exit_ref.shape[1:], jnp.float32), unroll=8)


def strips_pass(absorbers_ref, cross_ref, pass_ref, half, group):
    strips, cells = absorbers_ref.shape
    y = lax.broadcasted_iota(jnp.int32, (ROWS, cells), 0) + half * ROWS
    mine = lax.rem(lax.broadcasted_iota(jnp.int32, (ROWS, cells), 1), NY) == y
    cross = cross_ref[pl.ds(group, 1), :]
    for s in range(strips):
        depth = jnp.sum(jnp.where(mine, absorbers_ref[s : s + 1, :], 0.0), axis=1, keepdims=True)
        pass_ref[s] = jnp.exp(-(depth * cross))


def scan_kernel(axis, make_pass, exit_ref, *refs):
    groups = 16
    me = lax.axis_index(axis)
    group = lax.rem(me, groups)
    half = lax.rem(me // groups, NY // ROWS)
    way = me // (groups * (NY // ROWS))
    if make_pass:
        absorbers_ref, cross_ref, enter_ref, pass_ref = refs
        strips_pass(absorbers_ref, cross_ref, pass_ref, half, group)
    else:
        pass_ref, enter_ref = refs
    scan(exit_ref, pass_ref, enter_ref, way)


def rate_kernel(pattern_ref, q_ref, table_ref, bracket_ref, out_ref):
    r = pl.program_id(0)
    count = table_ref.shape[2]
    picked = jnp.concatenate(
        [
            q_ref[:, pl.ds(pl.multiple_of(pattern_ref[r, k] * LANES, LANES), LANES)]
            for k in range(count)
        ],
        axis=1,
    )
    both = jnp.concatenate(
        [
            jnp.concatenate([table_ref[b, 0, k] for k in range(count)], axis=1)
            for b in range(table_ref.shape[0])
        ],
        axis=0,
    )
    product = lax.dot_general(
        picked, both, (((1,), (1,)), ((), ())), preferred_element_type=jnp.float32
    )
    bracket = column(bracket_ref[...])
    out_ref[...] = jnp.where(bracket == 0, product[:, :LANES], product[:, LANES:])


def step_kernel(
    final, axis, *refs
):
    (p_ref, rate_ref, enter_ref, arrived_ref, inflow_ref, cross_ref, emission_ref,
     absorber_ref, stream_ref, crossways_ref) = refs[:10]
    absorber = column(absorber_ref[...])
    along_x = layers(column(stream_ref[...]))
    along_y = column(crossways_ref[...])
    forward_y = layers(jnp.maximum(along_y, 0.0))
    backward_y = layers(jnp.minimum(along_y, 0.0))
    inlet = lax.axis_index(axis) == 0
    groups = p_ref.shape[1] // LANES
    for g in range(groups):
        at = slice(g * LANES, (g + 1) * LANES)
        p = layers(p_ref[:, at])
        emission = emission_ref[:, at]
        emitted = [value * emission for value in p]
        passed = layers(jnp.exp(-(absorber * cross_ref[:, at])))
        absorbed = absorbed_of(passed, emitted, *get_enters(enter_ref, g, groups))
        boundary = jnp.where(inlet, inflow_ref[:, at], arrived_ref[:, at].astype(jnp.float32))
        carried = advection(p, boundary, along_x, forward_y, backward_y)
        rates = layers(rate_ref[:, at])
        tendency = [q - e + a + v for q, e, a, v in zip(rates, emitted, absorbed, carried)]
        if final:
            start_ref, updated_ref, absorption_ref = refs[10:]
            start = layers(start_ref[:, at])
            for k, rate in enumerate(tendency):
                here = slice(k * NY, (k + 1) * NY)
                updated_ref[here, at] = 0.5 * (start[k] + p[k] + time_step * rate)
                absorption_ref[here, at] = absorbed[k]
        else:
            middle_ref, q_ref, last_ref, exit_ref = refs[10:]
            middle = [value + time_step * rate for value, rate in zip(p, tendency)]
            for k, value in enumerate(middle):
                here = slice(k * NY, (k + 1) * NY)
                middle_ref[here, at] = value
                q_ref[here, at] = value.astype(jnp.bfloat16)
            last_ref[:, at] = middle[-1].astype(jnp.bfloat16)
            put_exits(exit_ref, g, groups, *exits(passed, [value * emission for value in middle]))


def vmem(count):
    return [pl.BlockSpec(memory_space=pltpu.VMEM)] * count


LIMIT = pltpu.CompilerParams(vmem_limit_bytes=48 * 2**20)


def call(body, args, outs, cost):
    return pl.pallas_call(
        body,
        out_shape=outs,
        in_specs=vmem(len(args)),
        out_specs=vmem(len(outs)),
        compiler_params=LIMIT,
        cost_estimate=pl.CostEstimate(flops=cost, bytes_accessed=cost, transcendentals=0),
    )(*args)


def rate_term(q, rate_blocks, pattern, bracket):
    cells = q.shape[0]
    brackets, rows, count, block, _ = rate_blocks.shape
    return pl.pallas_call(
        rate_kernel,
        grid_spec=pltpu.PrefetchScalarGridSpec(
            num_scalar_prefetch=1,
            grid=(rows,),
            in_specs=[
                pl.BlockSpec(q.shape, lambda r, pattern: (0, 0)),
                pl.BlockSpec((brackets, 1, count, block, block), lambda r, pattern: (0, r, 0, 0, 0)),
                pl.BlockSpec(bracket.shape, lambda r, pattern: (0, 0)),
            ],
            out_specs=pl.BlockSpec((cells, block), lambda r, pattern: (0, r)),
        ),
        out_shape=jax.ShapeDtypeStruct((cells, rows * block), jnp.float32),
        compiler_params=LIMIT,
        cost_estimate=pl.CostEstimate(
            flops=2 * cells * rate_blocks.size, bytes_accessed=2 * rate_blocks.size, transcendentals=0
        ),
    )(pattern, q, rate_blocks, bracket)


def shifted(value, axis):
    peers = lax.axis_size(axis)
    return lax.ppermute(value, axis, [(i, i + 1) for i in range(peers - 1)])


def local(
    populations,
    rate_blocks,
    pattern,
    bracket,
    cross_section,
    emission,
    absorber,
    stream_speed,
    cross_speed,
    inflow,
):
    cells, levels = populations.shape
    strips = lax.axis_size("cell")
    absorbers = lax.all_gather(absorber, "cell")
    bracket = bracket.reshape(1, cells)
    cross = cross_section.reshape(1, levels)
    crosses = cross_section.reshape(levels // LANES, LANES)
    emission = emission.reshape(1, levels)
    absorber = absorber.reshape(1, cells)
    stream = stream_speed.reshape(1, cells)
    crossways = cross_speed.reshape(1, cells)

    field = jax.ShapeDtypeStruct((cells, levels), jnp.float32)
    rounded = jax.ShapeDtypeStruct((cells, levels), jnp.bfloat16)
    layer = jax.ShapeDtypeStruct((NY, levels), jnp.bfloat16)
    tiles = jax.ShapeDtypeStruct((strips, ROWS, LANES), jnp.float32)
    size = cells * levels * 4

    def swap(value):
        return lax.all_to_all(value, "cell", 0, 0, tiled=True)

    q, last, leaving = call(
        first_kernel, (populations, cross, emission, absorber), (rounded, layer, tiles), 3 * size
    )
    gathered = lax.all_gather(q, "lev", axis=1, tiled=True)
    arrived = shifted(last, "cell")
    entering, passes = call(
        functools.partial(scan_kernel, "cell", True), (swap(leaving), absorbers, crosses), (tiles, tiles), size
    )
    entering = swap(entering)
    rates = rate_term(gathered, rate_blocks, pattern, bracket)
    middle, q, last, leaving = call(
        functools.partial(step_kernel, False, "cell"),
        (populations, rates, entering, arrived, inflow, cross, emission, absorber, stream, crossways),
        (field, rounded, layer, tiles),
        5 * size,
    )
    gathered = lax.all_gather(q, "lev", axis=1, tiled=True)
    arrived = shifted(last, "cell")
    (entering,) = call(
        functools.partial(scan_kernel, "cell", False), (swap(leaving), passes), (tiles,), size
    )
    entering = swap(entering)
    rates = rate_term(gathered, rate_blocks, pattern, bracket)
    return call(
        functools.partial(step_kernel, True, "cell"),
        (middle, rates, entering, arrived, inflow, cross, emission, absorber, stream, crossways, populations),
        (field, field),
        5 * size,
    )


def solution(mesh):
    in_specs = (
        P("cell", "lev"),
        P(None, "lev", None, None, None),
        P("lev", None),
        P("cell"),
        P("lev"),
        P("lev"),
        P("cell"),
        P("cell"),
        P("cell"),
        P(None, "lev"),
    )
    out_specs = (P("cell", "lev"), P("cell", "lev"))
    return jax.shard_map(local, mesh=mesh, in_specs=in_specs, out_specs=out_specs, check_vma=False)
```

```python
import functools

import jax
import jax.numpy as jnp
from jax import lax
from jax.experimental import pallas as pl
from jax.experimental.pallas import tpu as pltpu
from jax.sharding import PartitionSpec as P

NY = 16
LANES = 128
ROWS = 8
time_step = 0.25


def column(row):
    n = row.shape[1]
    at_row = lax.broadcasted_iota(jnp.int32, (n, n), 0)
    at_column = lax.broadcasted_iota(jnp.int32, (n, n), 1)
    return jnp.sum(jnp.where(at_row == at_column, row, jnp.zeros_like(row)), axis=1, keepdims=True)


def layers(value):
    return [value[k : k + NY] for k in range(0, value.shape[0], NY)]


def exits(passed, emitted):
    down, up = emitted[0], emitted[-1]
    for t, e in zip(passed[1:], emitted[1:]):
        down = t * down + e
    for t, e in zip(passed[-2::-1], emitted[-2::-1]):
        up = t * up + e
    return down, up


def put_exits(exit_ref, group, groups, down, up, depths=None):
    for way, value in enumerate((down, up)):
        for half in range(NY // ROWS):
            at = (way * (NY // ROWS) + half) * groups + group
            part = value[half * ROWS : (half + 1) * ROWS]
            if depths is not None:
                part = jnp.concatenate([part, depths[half]], axis=0).astype(exit_ref.dtype)
            exit_ref[at] = part


def get_enters(enter_ref, group, groups):
    found = []
    for way in range(2):
        halves = [
            enter_ref[(way * (NY // ROWS) + half) * groups + group]
            for half in range(NY // ROWS)
        ]
        found.append(jnp.concatenate(halves, axis=0))
    return found


def depth_tiles(absorber):
    total = sum(layers(absorber))
    high = total.astype(jnp.bfloat16).astype(jnp.float32)
    middle = (total - high).astype(jnp.bfloat16).astype(jnp.float32)
    low = total - high - middle
    lane = lax.broadcasted_iota(jnp.int32, (NY, LANES), 1)
    spread = jnp.where(lane == 0, high, jnp.where(lane == 1, middle, jnp.where(lane == 2, low, 0.0)))
    return [spread[half * ROWS : (half + 1) * ROWS] for half in range(NY // ROWS)]


def absorbed_of(passed, emitted, enter_down, enter_up):
    count = len(passed)
    downward, upward = [None] * count, [None] * count
    running = enter_down
    for k in range(count):
        running = passed[k] * running + emitted[k]
        downward[k] = running
    running = enter_up
    for k in reversed(range(count)):
        running = passed[k] * running + emitted[k]
        upward[k] = running
    return [
        (1.0 - t) * (d + u - 2.0 * e) for t, d, u, e in zip(passed, downward, upward, emitted)
    ]


def advection(layered, boundary, along_x, forward_y, backward_y):
    result, upstream = [], boundary
    for k, here in enumerate(layered):
        before = pltpu.roll(here, 1, 0)
        after = pltpu.roll(here, NY - 1, 0)
        result.append(
            -along_x[k] * (here - upstream) - forward_y[k] * (here - before) - backward_y[k] * (after - here)
        )
        upstream = here
    return result


def first_kernel(p_hbm, cross_hbm, emission_hbm, absorber_hbm, q_ref, last_ref, exit_ref, *scratch):
    sems = scratch[-1]
    copies = [
        pltpu.make_async_copy(source, target, sems.at[i])
        for i, (source, target) in enumerate(
            zip((p_hbm, cross_hbm, emission_hbm, absorber_hbm), scratch[:-1])
        )
    ]
    for copy in copies:
        copy.start()
    for copy in copies:
        copy.wait()
    p_ref, cross_ref, emission_ref, absorber_ref = scratch[:-1]
    absorber = column(absorber_ref[...])
    depths = depth_tiles(absorber)
    groups = p_ref.shape[1] // LANES
    for g in range(groups):
        at = slice(g * LANES, (g + 1) * LANES)
        p = p_ref[:, at]
        q = p.astype(jnp.bfloat16)
        q_ref[:, at] = q
        last_ref[:, at] = q[-NY:]
        passed = layers(jnp.exp(-(absorber * cross_ref[:, at])))
        emitted = layers(p * emission_ref[:, at])
        put_exits(exit_ref, g, groups, *exits(passed, emitted), depths)


def scan(exits_in, pass_ref, enter_ref, way):
    count = enter_ref.shape[0]

    def step(i, carry):
        at = jnp.where(way == 0, i, count - 1 - i)
        enter_ref[at] = carry
        return pass_ref[at] * carry + exits_in(at)

    lax.fori_loop(0, count, step, jnp.zeros(enter_ref.shape[1:], jnp.float32), unroll=8)


def first_scan_kernel(axis, arrived_ref, cross_ref, enter_ref, pass_ref, exit_ref):
    groups = cross_ref.shape[0]
    me = lax.axis_index(axis)
    cross = cross_ref[pl.ds(lax.rem(me, groups), 1), :]
    for s in range(arrived_ref.shape[0]):
        arrived = arrived_ref[s].astype(jnp.float32)
        exit_ref[s] = arrived[:ROWS]
        depth = jnp.sum(arrived[ROWS:], axis=1, keepdims=True)
        pass_ref[s] = jnp.exp(-(depth * cross))
    scan(lambda at: exit_ref[at], pass_ref, enter_ref, me // (groups * (NY // ROWS)))


def second_scan_kernel(axis, groups, exit_ref, pass_ref, enter_ref):
    scan(lambda at: exit_ref[at], pass_ref, enter_ref, lax.axis_index(axis) // (groups * (NY // ROWS)))


def rate_kernel(pattern_ref, q_ref, table_ref, bracket_ref, out_ref):
    brackets, rows, count = table_ref.shape[:3]
    bracket = column(bracket_ref[...])
    for row in range(rows):
        r = pl.program_id(0) * rows + row
        picked = jnp.concatenate(
            [
                q_ref[:, pl.ds(pl.multiple_of(pattern_ref[r, k] * LANES, LANES), LANES)]
                for k in range(count)
            ],
            axis=1,
        )
        both = jnp.concatenate(
            [
                jnp.concatenate([table_ref[b, row, k] for k in range(count)], axis=1)
                for b in range(brackets)
            ],
            axis=0,
        )
        product = lax.dot_general(
            picked, both, (((1,), (1,)), ((), ())), preferred_element_type=jnp.float32
        )
        out_ref[:, row * LANES : (row + 1) * LANES] = jnp.where(
            bracket == 0, product[:, :LANES], product[:, LANES:]
        )


def step_kernel(final, axis, *refs):
    (p_ref, rate_ref, enter_ref, arrived_ref, inflow_ref, cross_ref, emission_ref,
     absorber_ref, stream_ref, crossways_ref) = refs[:10]
    absorber = column(absorber_ref[...])
    along_x = layers(column(stream_ref[...]))
    along_y = column(crossways_ref[...])
    forward_y = layers(jnp.maximum(along_y, 0.0))
    backward_y = layers(jnp.minimum(along_y, 0.0))
    inlet = lax.axis_index(axis) == 0
    groups = p_ref.shape[1] // LANES
    for g in range(groups):
        at = slice(g * LANES, (g + 1) * LANES)
        p = layers(p_ref[:, at])
        emission = emission_ref[:, at]
        emitted = [value * emission for value in p]
        passed = layers(jnp.exp(-(absorber * cross_ref[:, at])))
        absorbed = absorbed_of(passed, emitted, *get_enters(enter_ref, g, groups))
        boundary = jnp.where(inlet, inflow_ref[:, at], arrived_ref[:, at].astype(jnp.float32))
        carried = advection(p, boundary, along_x, forward_y, backward_y)
        rates = layers(rate_ref[:, at])
        tendency = [q - e + a + v for q, e, a, v in zip(rates, emitted, absorbed, carried)]
        if final:
            start_ref, updated_ref, absorption_ref = refs[10:]
            start = layers(start_ref[:, at])
            for k, rate in enumerate(tendency):
                here = slice(k * NY, (k + 1) * NY)
                updated_ref[here, at] = 0.5 * (start[k] + p[k] + time_step * rate)
                absorption_ref[here, at] = absorbed[k]
        else:
            middle_ref, q_ref, last_ref, exit_ref = refs[10:]
            middle = [value + time_step * rate for value, rate in zip(p, tendency)]
            for k, value in enumerate(middle):
                here = slice(k * NY, (k + 1) * NY)
                middle_ref[here, at] = value
                q_ref[here, at] = value.astype(jnp.bfloat16)
            last_ref[:, at] = middle[-1].astype(jnp.bfloat16)
            put_exits(exit_ref, g, groups, *exits(passed, [value * emission for value in middle]))


def vmem(count):
    return [pl.BlockSpec(memory_space=pltpu.VMEM)] * count


LIMIT = pltpu.CompilerParams(vmem_limit_bytes=48 * 2**20)


def call(body, args, outs, cost, scratch=(), in_specs=None):
    return pl.pallas_call(
        body,
        out_shape=outs,
        in_specs=in_specs or vmem(len(args)),
        out_specs=vmem(len(outs)),
        scratch_shapes=scratch,
        compiler_params=LIMIT,
        cost_estimate=pl.CostEstimate(flops=cost, bytes_accessed=cost, transcendentals=0),
    )(*args)


def rate_term(q, rate_blocks, pattern, bracket):
    cells = q.shape[0]
    brackets, rows, count, block, _ = rate_blocks.shape
    step = rows // 2
    return pl.pallas_call(
        rate_kernel,
        grid_spec=pltpu.PrefetchScalarGridSpec(
            num_scalar_prefetch=1,
            grid=(rows // step,),
            in_specs=[
                pl.BlockSpec(q.shape, lambda r, pattern: (0, 0)),
                pl.BlockSpec((brackets, step, count, block, block), lambda r, pattern: (0, r, 0, 0, 0)),
                pl.BlockSpec(bracket.shape, lambda r, pattern: (0, 0)),
            ],
            out_specs=pl.BlockSpec((cells, step * block), lambda r, pattern: (0, r)),
        ),
        out_shape=jax.ShapeDtypeStruct((cells, rows * block), jnp.float32),
        compiler_params=LIMIT,
        cost_estimate=pl.CostEstimate(
            flops=2 * cells * rate_blocks.size, bytes_accessed=2 * rate_blocks.size, transcendentals=0
        ),
    )(pattern, q, rate_blocks, bracket)


def shifted(value, axis):
    peers = lax.axis_size(axis)
    return lax.ppermute(value, axis, [(i, i + 1) for i in range(peers - 1)])


def local(
    populations,
    rate_blocks,
    pattern,
    bracket,
    cross_section,
    emission,
    absorber,
    stream_speed,
    cross_speed,
    inflow,
):
    cells, levels = populations.shape
    strips = lax.axis_size("cell")
    bracket = bracket.reshape(1, cells)
    cross = cross_section.reshape(1, levels)
    crosses = cross_section.reshape(levels // LANES, LANES)
    emission = emission.reshape(1, levels)
    absorber = absorber.reshape(1, cells)
    stream = stream_speed.reshape(1, cells)
    crossways = cross_speed.reshape(1, cells)

    field = jax.ShapeDtypeStruct((cells, levels), jnp.float32)
    rounded = jax.ShapeDtypeStruct((cells, levels), jnp.bfloat16)
    layer = jax.ShapeDtypeStruct((NY, levels), jnp.bfloat16)
    tiles = jax.ShapeDtypeStruct((strips, ROWS, LANES), jnp.float32)
    size = cells * levels * 4

    def swap(value):
        return lax.all_to_all(value, "cell", 0, 0, tiled=True)

    sources = (populations, cross, emission, absorber)
    q, last, leaving = call(
        first_kernel,
        sources,
        (rounded, layer, jax.ShapeDtypeStruct((strips, 2 * ROWS, LANES), jnp.bfloat16)),
        3 * size,
        [pltpu.VMEM(value.shape, value.dtype) for value in sources]
        + [pltpu.SemaphoreType.DMA((len(sources),))],
        [pl.BlockSpec(memory_space=pl.ANY)] * len(sources),
    )
    gathered = lax.all_gather(q, "lev", axis=1, tiled=True)
    arrived = shifted(last, "cell")
    entering, passes = call(
        functools.partial(first_scan_kernel, "cell"),
        (swap(leaving), crosses),
        (tiles, tiles),
        size,
        [pltpu.VMEM(tiles.shape, jnp.float32)],
    )
    entering = swap(entering)
    rates = rate_term(gathered, rate_blocks, pattern, bracket)
    middle, q, last, leaving = call(
        functools.partial(step_kernel, False, "cell"),
        (populations, rates, entering, arrived, inflow, cross, emission, absorber, stream, crossways),
        (field, rounded, layer, tiles),
        5 * size,
    )
    gathered = lax.all_gather(q, "lev", axis=1, tiled=True)
    arrived = shifted(last, "cell")
    (entering,) = call(
        functools.partial(second_scan_kernel, "cell", levels // LANES), (swap(leaving), passes), (tiles,), size
    )
    entering = swap(entering)
    rates = rate_term(gathered, rate_blocks, pattern, bracket)
    return call(
        functools.partial(step_kernel, True, "cell"),
        (middle, rates, entering, arrived, inflow, cross, emission, absorber, stream, crossways, populations),
        (field, field),
        5 * size,
    )


def solution(mesh):
    in_specs = (
        P("cell", "lev"),
        P(None, "lev", None, None, None),
        P("lev", None),
        P("cell"),
        P("lev"),
        P("lev"),
        P("cell"),
        P("cell"),
        P("cell"),
        P(None, "lev"),
    )
    out_specs = (P("cell", "lev"), P("cell", "lev"))
    return jax.shard_map(local, mesh=mesh, in_specs=in_specs, out_specs=out_specs, check_vma=False)
```

```python
import functools

import jax
import jax.numpy as jnp
from jax import lax
from jax.experimental import pallas as pl
from jax.experimental.pallas import tpu as pltpu
from jax.sharding import PartitionSpec as P

NY = 16
LANES = 128
ROWS = 8
time_step = 0.25


def column(row):
    n = row.shape[1]
    at_row = lax.broadcasted_iota(jnp.int32, (n, n), 0)
    at_column = lax.broadcasted_iota(jnp.int32, (n, n), 1)
    return jnp.sum(jnp.where(at_row == at_column, row, jnp.zeros_like(row)), axis=1, keepdims=True)


def layers(value):
    return [value[k : k + NY] for k in range(0, value.shape[0], NY)]


def exits(passed, emitted):
    down, up = emitted[0], emitted[-1]
    for t, e in zip(passed[1:], emitted[1:]):
        down = t * down + e
    for t, e in zip(passed[-2::-1], emitted[-2::-1]):
        up = t * up + e
    return down, up


def put_exits(exit_ref, group, groups, down, up, depths=None):
    for way, value in enumerate((down, up)):
        for half in range(NY // ROWS):
            at = (way * (NY // ROWS) + half) * groups + group
            part = value[half * ROWS : (half + 1) * ROWS]
            if depths is not None:
                part = jnp.concatenate([part, depths[half]], axis=0).astype(exit_ref.dtype)
            exit_ref[at] = part


def get_enters(enter_ref, group, groups):
    found = []
    for way in range(2):
        halves = [
            enter_ref[(way * (NY // ROWS) + half) * groups + group]
            for half in range(NY // ROWS)
        ]
        found.append(jnp.concatenate(halves, axis=0))
    return found


def depth_tiles(absorber):
    total = sum(layers(absorber))
    high = total.astype(jnp.bfloat16).astype(jnp.float32)
    middle = (total - high).astype(jnp.bfloat16).astype(jnp.float32)
    low = total - high - middle
    lane = lax.broadcasted_iota(jnp.int32, (NY, LANES), 1)
    spread = jnp.where(lane == 0, high, jnp.where(lane == 1, middle, jnp.where(lane == 2, low, 0.0)))
    return [spread[half * ROWS : (half + 1) * ROWS] for half in range(NY // ROWS)]


def absorbed_of(passed, emitted, enter_down, enter_up):
    count = len(passed)
    downward, upward = [None] * count, [None] * count
    running = enter_down
    for k in range(count):
        running = passed[k] * running + emitted[k]
        downward[k] = running
    running = enter_up
    for k in reversed(range(count)):
        running = passed[k] * running + emitted[k]
        upward[k] = running
    return [
        (1.0 - t) * (d + u - 2.0 * e) for t, d, u, e in zip(passed, downward, upward, emitted)
    ]


def advection(layered, boundary, along_x, forward_y, backward_y):
    result, upstream = [], boundary
    for k, here in enumerate(layered):
        before = pltpu.roll(here, 1, 0)
        after = pltpu.roll(here, NY - 1, 0)
        result.append(
            -along_x[k] * (here - upstream) - forward_y[k] * (here - before) - backward_y[k] * (after - here)
        )
        upstream = here
    return result


def first_kernel(p_hbm, cross_hbm, emission_hbm, absorber_hbm, q_ref, last_ref, exit_ref, *scratch):
    sems = scratch[-1]
    copies = [
        pltpu.make_async_copy(source, target, sems.at[i])
        for i, (source, target) in enumerate(
            zip((p_hbm, cross_hbm, emission_hbm, absorber_hbm), scratch[:-1])
        )
    ]
    for copy in copies:
        copy.start()
    for copy in copies:
        copy.wait()
    p_ref, cross_ref, emission_ref, absorber_ref = scratch[:-1]
    absorber = column(absorber_ref[...])
    depths = depth_tiles(absorber)
    groups = p_ref.shape[1] // LANES
    for g in range(groups):
        at = slice(g * LANES, (g + 1) * LANES)
        p = p_ref[:, at]
        q = p.astype(jnp.bfloat16)
        q_ref[:, at] = q
        last_ref[:, at] = q[-NY:]
        passed = layers(jnp.exp(-(absorber * cross_ref[:, at])))
        emitted = layers(p * emission_ref[:, at])
        put_exits(exit_ref, g, groups, *exits(passed, emitted), depths)


def scan(exits_in, pass_ref, enter_ref, way):
    count = enter_ref.shape[0]

    def step(i, carry):
        at = jnp.where(way == 0, i, count - 1 - i)
        enter_ref[at] = carry
        return pass_ref[at] * carry + exits_in(at)

    lax.fori_loop(0, count, step, jnp.zeros(enter_ref.shape[1:], jnp.float32), unroll=8)


def first_scan_kernel(axis, arrived_ref, cross_ref, enter_ref, pass_ref, exit_ref):
    groups = cross_ref.shape[0]
    me = lax.axis_index(axis)
    cross = cross_ref[pl.ds(lax.rem(me, groups), 1), :]
    for s in range(arrived_ref.shape[0]):
        arrived = arrived_ref[s].astype(jnp.float32)
        exit_ref[s] = arrived[:ROWS]
        depth = jnp.sum(arrived[ROWS:], axis=1, keepdims=True)
        pass_ref[s] = jnp.exp(-(depth * cross))
    scan(lambda at: exit_ref[at], pass_ref, enter_ref, me // (groups * (NY // ROWS)))


def second_scan_kernel(axis, groups, exit_ref, pass_ref, enter_ref):
    scan(lambda at: exit_ref[at], pass_ref, enter_ref, lax.axis_index(axis) // (groups * (NY // ROWS)))


def rate_kernel(axis, pattern_ref, *refs):
    pieces, (table_ref, bracket_ref, out_ref, q_ref) = refs[:-4], refs[-4:]
    brackets, rows, count = table_ref.shape[:3]
    width = pieces[0].shape[1]
    for place, piece in enumerate(pieces):
        q_ref[:, place * width : (place + 1) * width] = piece[...]
    me = lax.axis_index(axis)
    bracket = column(bracket_ref[...])

    def block(r, k):
        source = pattern_ref[r, k]
        place = lax.rem(source, rows) + rows * ((source // rows) ^ me)
        return q_ref[:, pl.ds(pl.multiple_of(place * LANES, LANES), LANES)]

    for r in range(rows):
        picked = jnp.concatenate([block(r, k) for k in range(count)], axis=1)
        both = jnp.concatenate(
            [
                jnp.concatenate([table_ref[b, r, k] for k in range(count)], axis=1)
                for b in range(brackets)
            ],
            axis=0,
        )
        product = lax.dot_general(
            picked, both, (((1,), (1,)), ((), ())), preferred_element_type=jnp.float32
        )
        out_ref[:, r * LANES : (r + 1) * LANES] = jnp.where(
            bracket == 0, product[:, :LANES], product[:, LANES:]
        )


def step_kernel(final, axis, *refs):
    (p_ref, rate_ref, enter_ref, arrived_ref, inflow_ref, cross_ref, emission_ref,
     absorber_ref, stream_ref, crossways_ref) = refs[:10]
    absorber = column(absorber_ref[...])
    along_x = layers(column(stream_ref[...]))
    along_y = column(crossways_ref[...])
    forward_y = layers(jnp.maximum(along_y, 0.0))
    backward_y = layers(jnp.minimum(along_y, 0.0))
    inlet = lax.axis_index(axis) == 0
    groups = p_ref.shape[1] // LANES
    for g in range(groups):
        at = slice(g * LANES, (g + 1) * LANES)
        p = layers(p_ref[:, at])
        emission = emission_ref[:, at]
        emitted = [value * emission for value in p]
        passed = layers(jnp.exp(-(absorber * cross_ref[:, at])))
        absorbed = absorbed_of(passed, emitted, *get_enters(enter_ref, g, groups))
        boundary = jnp.where(inlet, inflow_ref[:, at], arrived_ref[:, at].astype(jnp.float32))
        carried = advection(p, boundary, along_x, forward_y, backward_y)
        rates = layers(rate_ref[:, at])
        tendency = [q - e + a + v for q, e, a, v in zip(rates, emitted, absorbed, carried)]
        if final:
            start_ref, updated_ref, absorption_ref = refs[10:]
            start = layers(start_ref[:, at])
            for k, rate in enumerate(tendency):
                here = slice(k * NY, (k + 1) * NY)
                updated_ref[here, at] = 0.5 * (start[k] + p[k] + time_step * rate)
                absorption_ref[here, at] = absorbed[k]
        else:
            middle_ref, q_ref, last_ref, exit_ref = refs[10:]
            middle = [value + time_step * rate for value, rate in zip(p, tendency)]
            for k, value in enumerate(middle):
                here = slice(k * NY, (k + 1) * NY)
                middle_ref[here, at] = value
                q_ref[here, at] = value.astype(jnp.bfloat16)
            last_ref[:, at] = middle[-1].astype(jnp.bfloat16)
            put_exits(exit_ref, g, groups, *exits(passed, [value * emission for value in middle]))


def vmem(count):
    return [pl.BlockSpec(memory_space=pltpu.VMEM)] * count


LIMIT = pltpu.CompilerParams(vmem_limit_bytes=24 * 2**20)


def call(body, args, outs, cost, scratch=(), in_specs=None):
    return pl.pallas_call(
        body,
        out_shape=outs,
        in_specs=in_specs or vmem(len(args)),
        out_specs=vmem(len(outs)),
        scratch_shapes=scratch,
        compiler_params=LIMIT,
        cost_estimate=pl.CostEstimate(flops=cost, bytes_accessed=cost, transcendentals=0),
    )(*args)


def gathered(q, axis):
    def swap(value, apart):
        return lax.ppermute(value, axis, [(i, i ^ apart) for i in range(lax.axis_size(axis))])

    far = swap(q, 2)
    return q, swap(q, 1), far, swap(far, 1)


def rate_term(pieces, rate_blocks, pattern, bracket):
    cells, levels = pieces[0].shape
    return pl.pallas_call(
        functools.partial(rate_kernel, "lev"),
        in_specs=[pl.BlockSpec(memory_space=pltpu.SMEM)] + vmem(len(pieces) + 2),
        out_specs=pl.BlockSpec(memory_space=pltpu.VMEM),
        out_shape=jax.ShapeDtypeStruct((cells, levels), jnp.float32),
        scratch_shapes=[pltpu.VMEM((cells, len(pieces) * levels), jnp.bfloat16)],
        compiler_params=LIMIT,
        cost_estimate=pl.CostEstimate(
            flops=2 * cells * rate_blocks.size, bytes_accessed=2 * rate_blocks.size, transcendentals=0
        ),
    )(pattern, *pieces, rate_blocks, bracket)


def shifted(value, axis):
    peers = lax.axis_size(axis)
    return lax.ppermute(value, axis, [(i, i + 1) for i in range(peers - 1)])


def local(
    populations,
    rate_blocks,
    pattern,
    bracket,
    cross_section,
    emission,
    absorber,
    stream_speed,
    cross_speed,
    inflow,
):
    cells, levels = populations.shape
    strips = lax.axis_size("cell")
    bracket = bracket.reshape(1, cells)
    cross = cross_section.reshape(1, levels)
    crosses = cross_section.reshape(levels // LANES, LANES)
    emission = emission.reshape(1, levels)
    absorber = absorber.reshape(1, cells)
    stream = stream_speed.reshape(1, cells)
    crossways = cross_speed.reshape(1, cells)

    field = jax.ShapeDtypeStruct((cells, levels), jnp.float32)
    rounded = jax.ShapeDtypeStruct((cells, levels), jnp.bfloat16)
    layer = jax.ShapeDtypeStruct((NY, levels), jnp.bfloat16)
    tiles = jax.ShapeDtypeStruct((strips, ROWS, LANES), jnp.float32)
    size = cells * levels * 4

    def swap(value):
        return lax.all_to_all(value, "cell", 0, 0, tiled=True)

    sources = (populations, cross, emission, absorber)
    q, last, leaving = call(
        first_kernel,
        sources,
        (rounded, layer, jax.ShapeDtypeStruct((strips, 2 * ROWS, LANES), jnp.bfloat16)),
        3 * size,
        [pltpu.VMEM(value.shape, value.dtype) for value in sources]
        + [pltpu.SemaphoreType.DMA((len(sources),))],
        [pl.BlockSpec(memory_space=pltpu.HBM)] * len(sources),
    )
    pieces = gathered(q, "lev")
    arrived = shifted(last, "cell")
    entering, passes = call(
        functools.partial(first_scan_kernel, "cell"),
        (swap(leaving), crosses),
        (tiles, tiles),
        size,
        [pltpu.VMEM(tiles.shape, jnp.float32)],
    )
    entering = swap(entering)
    rates = rate_term(pieces, rate_blocks, pattern, bracket)
    middle, q, last, leaving = call(
        functools.partial(step_kernel, False, "cell"),
        (populations, rates, entering, arrived, inflow, cross, emission, absorber, stream, crossways),
        (field, rounded, layer, tiles),
        5 * size,
    )
    pieces = gathered(q, "lev")
    arrived = shifted(last, "cell")
    (entering,) = call(
        functools.partial(second_scan_kernel, "cell", levels // LANES), (swap(leaving), passes), (tiles,), size
    )
    entering = swap(entering)
    rates = rate_term(pieces, rate_blocks, pattern, bracket)
    return call(
        functools.partial(step_kernel, True, "cell"),
        (middle, rates, entering, arrived, inflow, cross, emission, absorber, stream, crossways, populations),
        (field, field),
        5 * size,
    )


def solution(mesh):
    in_specs = (
        P("cell", "lev"),
        P(None, "lev", None, None, None),
        P("lev", None),
        P("cell"),
        P("lev"),
        P("lev"),
        P("cell"),
        P("cell"),
        P("cell"),
        P(None, "lev"),
    )
    out_specs = (P("cell", "lev"), P("cell", "lev"))
    return jax.shard_map(local, mesh=mesh, in_specs=in_specs, out_specs=out_specs, check_vma=False)
```

```python
import functools

import jax
import jax.numpy as jnp
from jax import lax
from jax.experimental import pallas as pl
from jax.experimental.pallas import tpu as pltpu
from jax.sharding import PartitionSpec as P

NY = 16
LANES = 128
ROWS = 8
HALF = 4
PARTS = 3
time_step = 0.25


def column(row):
    n = row.shape[1]
    at_row = lax.broadcasted_iota(jnp.int32, (n, n), 0)
    at_column = lax.broadcasted_iota(jnp.int32, (n, n), 1)
    return jnp.sum(jnp.where(at_row == at_column, row, jnp.zeros_like(row)), axis=1, keepdims=True)


def layers(value):
    return [value[k : k + NY] for k in range(0, value.shape[0], NY)]


def exits(passed, emitted):
    down, up = emitted[0], emitted[-1]
    for t, e in zip(passed[1:], emitted[1:]):
        down = t * down + e
    for t, e in zip(passed[-2::-1], emitted[-2::-1]):
        up = t * up + e
    return down, up


def top(value):
    return lax.broadcasted_iota(jnp.int32, value.shape, 0) < HALF


def to_tiles(down, up):
    tiles = []
    for k in range(0, NY, ROWS):
        d, u = down[k : k + ROWS], up[k : k + ROWS]
        tiles.append(jnp.where(top(d), d, pltpu.roll(u, HALF, 0)))
        tiles.append(jnp.where(top(d), pltpu.roll(d, HALF, 0), u))
    return tiles


def from_tiles(tiles):
    down, up = [], []
    for first, second in zip(tiles[::2], tiles[1::2]):
        down.append(jnp.where(top(first), first, pltpu.roll(second, HALF, 0)))
        up.append(jnp.where(top(first), pltpu.roll(first, HALF, 0), second))
    return jnp.concatenate(down, axis=0), jnp.concatenate(up, axis=0)


def get_enters(enter_ref, group, groups):
    return from_tiles([enter_ref[k * groups + group, :ROWS] for k in range(NY // HALF)])


def depth_tiles(absorber):
    lane = lax.broadcasted_iota(jnp.int32, (NY, LANES), 1)
    by_layer = layers(absorber)
    count = len(by_layer)
    forward = reverse = jnp.zeros((NY, LANES), jnp.float32)
    for k, value in enumerate(by_layer):
        high = value.astype(jnp.bfloat16).astype(jnp.float32)
        middle = (value - high).astype(jnp.bfloat16).astype(jnp.float32)
        for j, part in enumerate((high, middle, value - high - middle)):
            forward = jnp.where(lane == PARTS * k + j, part, forward)
            reverse = jnp.where(lane == PARTS * (count - 1 - k) + j, part, reverse)
    return to_tiles(forward, reverse)


def absorbed_of(passed, emitted, enter_down, enter_up):
    count = len(passed)
    downward, upward = [None] * count, [None] * count
    running = enter_down
    for k in range(count):
        running = emitted[k] if running is None else passed[k] * running + emitted[k]
        downward[k] = running
    running = enter_up
    for k in reversed(range(count)):
        running = emitted[k] if running is None else passed[k] * running + emitted[k]
        upward[k] = running
    return [
        (1.0 - t) * (d + u - 2.0 * e) for t, d, u, e in zip(passed, downward, upward, emitted)
    ]


def advection(layered, boundary, along_x, forward_y, backward_y):
    result, upstream = [], boundary
    for k, here in enumerate(layered):
        before = pltpu.roll(here, 1, 0)
        after = pltpu.roll(here, NY - 1, 0)
        result.append(
            -along_x[k] * (here - upstream) - forward_y[k] * (here - before) - backward_y[k] * (after - here)
        )
        upstream = here
    return result


def first_kernel(p_hbm, cross_hbm, emission_hbm, absorber_hbm, q_ref, last_ref, exit_ref, *scratch):
    sems = scratch[-1]
    copies = [
        pltpu.make_async_copy(source, target, sems.at[i])
        for i, (source, target) in enumerate(
            zip((p_hbm, cross_hbm, emission_hbm, absorber_hbm), scratch[:-1])
        )
    ]
    for copy in copies:
        copy.start()
    for copy in copies:
        copy.wait()
    p_ref, cross_ref, emission_ref, absorber_ref = scratch[:-1]
    absorber = column(absorber_ref[...])
    depths = depth_tiles(absorber)
    groups = p_ref.shape[1] // LANES
    for g in range(groups):
        at = slice(g * LANES, (g + 1) * LANES)
        p = p_ref[:, at]
        q = p.astype(jnp.bfloat16)
        q_ref[:, at] = q
        last_ref[:, at] = q[-NY:]
        passed = layers(jnp.exp(-(absorber * cross_ref[:, at])))
        emitted = layers(p * emission_ref[:, at])
        for k, (tile, depth) in enumerate(zip(to_tiles(*exits(passed, emitted)), depths)):
            exit_ref[k * groups + g] = jnp.concatenate([tile, depth], axis=0).astype(jnp.bfloat16)


def scan(exit_of, pass_ref, enter_ref):
    count = enter_ref.shape[0]
    carry = jnp.zeros(enter_ref.shape[1:], jnp.float32)
    upper = top(carry)
    for i in range(count):
        j = count - 1 - i
        enter_ref[i, :HALF] = carry[:HALF]
        enter_ref[j, HALF:] = carry[HALF:]
        carry = jnp.where(upper, pass_ref[i], pass_ref[j]) * carry + jnp.where(
            upper, exit_of(i), exit_of(j)
        )


def first_scan_kernel(axis, arrived_ref, cross_ref, enter_ref, pass_ref, exit_ref):
    group = lax.rem(lax.axis_index(axis), cross_ref.shape[0])
    cross = cross_ref[pl.ds(group, 1), :]
    for s in range(arrived_ref.shape[0]):
        arrived = arrived_ref[s].astype(jnp.float32)
        exit_ref[s] = arrived[:ROWS]
        depth = jnp.sum(arrived[ROWS:], axis=1, keepdims=True)
        pass_ref[s] = jnp.exp(-(depth * cross))
    scan(lambda at: exit_ref[at], pass_ref, enter_ref)


def response_kernel(axis, count, arrived_ref, cross_ref, emission_ref, same_ref, other_ref):
    group = lax.rem(lax.axis_index(axis), cross_ref.shape[0])
    cross = cross_ref[pl.ds(group, 1), :]
    emission = time_step * emission_ref[pl.ds(group, 1), :]
    lane = lax.broadcasted_iota(jnp.int32, (ROWS, LANES), 1)
    mine = [(lane >= PARTS * k) & (lane < PARTS * (k + 1)) for k in range(count)]
    for s in range(arrived_ref.shape[0]):
        depths = arrived_ref[s].astype(jnp.float32)[ROWS:]
        after = jnp.ones((ROWS, LANES), jnp.float32)
        taken = other = jnp.zeros((ROWS, LANES), jnp.float32)
        for k in reversed(range(count)):
            depth = jnp.sum(jnp.where(mine[k], depths, 0.0), axis=1, keepdims=True)
            t = jnp.exp(-(depth * cross))
            taken = taken + (1.0 - t)
            other = other + (after * after) * (t * (1.0 - t))
            after = after * t
        same_ref[s] = emission * (after * taken)
        other_ref[s] = emission * other


def second_scan_kernel(arrived_ref, entered_ref, pass_ref, same_ref, other_ref, enter_ref, exit_ref):
    for s in range(arrived_ref.shape[0]):
        entered = entered_ref[s]
        exit_ref[s] = (
            arrived_ref[s, ROWS:]
            + same_ref[s] * entered
            + other_ref[s] * pltpu.roll(entered, HALF, 0)
        )
    scan(lambda at: exit_ref[at], pass_ref, enter_ref)


def rate_kernel(axis, pattern_ref, *refs):
    pieces, (table_ref, bracket_ref, out_ref, q_ref) = refs[:-4], refs[-4:]
    brackets, rows, count = table_ref.shape[:3]
    width = pieces[0].shape[1]
    for place, piece in enumerate(pieces):
        q_ref[:, place * width : (place + 1) * width] = piece[...]
    me = lax.axis_index(axis)
    bracket = column(bracket_ref[...])

    def block(r, k):
        source = pattern_ref[r, k]
        place = lax.rem(source, rows) + rows * ((source // rows) ^ me)
        return q_ref[:, pl.ds(pl.multiple_of(place * LANES, LANES), LANES)]

    for r in range(rows):
        picked = jnp.concatenate([block(r, k) for k in range(count)], axis=1)
        both = jnp.concatenate(
            [
                jnp.concatenate([table_ref[b, r, k] for k in range(count)], axis=1)
                for b in range(brackets)
            ],
            axis=0,
        )
        product = lax.dot_general(
            picked, both, (((1,), (1,)), ((), ())), preferred_element_type=jnp.float32
        )
        out_ref[:, r * LANES : (r + 1) * LANES] = jnp.where(
            bracket == 0, product[:, :LANES], product[:, LANES:]
        )


def step_kernel(final, axis, *refs):
    (p_ref, rate_ref, enter_ref, arrived_ref, inflow_ref, cross_ref, emission_ref,
     absorber_ref, stream_ref, crossways_ref) = refs[:10]
    absorber = column(absorber_ref[...])
    along_x = layers(column(stream_ref[...]))
    along_y = column(crossways_ref[...])
    forward_y = layers(jnp.maximum(along_y, 0.0))
    backward_y = layers(jnp.minimum(along_y, 0.0))
    inlet = lax.axis_index(axis) == 0
    groups = p_ref.shape[1] // LANES
    for g in range(groups):
        at = slice(g * LANES, (g + 1) * LANES)
        p = layers(p_ref[:, at])
        emission = emission_ref[:, at]
        emitted = [value * emission for value in p]
        passed = layers(jnp.exp(-(absorber * cross_ref[:, at])))
        entering = get_enters(enter_ref, g, groups) if final else (None, None)
        absorbed = absorbed_of(passed, emitted, *entering)
        boundary = jnp.where(inlet, inflow_ref[:, at], arrived_ref[:, at].astype(jnp.float32))
        carried = advection(p, boundary, along_x, forward_y, backward_y)
        rates = layers(rate_ref[:, at])
        tendency = [q - e + a + v for q, e, a, v in zip(rates, emitted, absorbed, carried)]
        if final:
            start_ref, updated_ref, absorption_ref = refs[10:]
            start = layers(start_ref[:, at])
            for k, rate in enumerate(tendency):
                here = slice(k * NY, (k + 1) * NY)
                updated_ref[here, at] = 0.5 * (start[k] + p[k] + time_step * rate)
                absorption_ref[here, at] = absorbed[k]
        else:
            middle_ref, swap_ref = refs[10:]
            middle = [value + time_step * rate for value, rate in zip(p, tendency)]
            for k, value in enumerate(middle):
                middle_ref[k * NY : (k + 1) * NY, at] = value
            leaving = to_tiles(*exits(passed, [value * emission for value in middle]))
            for k, tile in enumerate(leaving):
                swap_ref[k * groups + g, :ROWS] = enter_ref[k * groups + g]
                swap_ref[k * groups + g, ROWS:] = tile


def middle_kernel(part_ref, swap_ref, cross_ref, absorber_ref, middle_ref, q_ref, last_ref):
    absorber = column(absorber_ref[...])
    groups = part_ref.shape[1] // LANES
    for g in range(groups):
        at = slice(g * LANES, (g + 1) * LANES)
        part = layers(part_ref[:, at])
        passed = layers(jnp.exp(-(absorber * cross_ref[:, at])))
        downward, upward = get_enters(swap_ref, g, groups)
        count = len(passed)
        down, up = [None] * count, [None] * count
        for k in range(count):
            downward = passed[k] * downward
            down[k] = downward
        for k in reversed(range(count)):
            upward = passed[k] * upward
            up[k] = upward
        for k in range(count):
            here = slice(k * NY, (k + 1) * NY)
            value = part[k] + time_step * ((1.0 - passed[k]) * (down[k] + up[k]))
            middle_ref[here, at] = value
            q_ref[here, at] = value.astype(jnp.bfloat16)
            if k == count - 1:
                last_ref[:, at] = value.astype(jnp.bfloat16)


def vmem(count):
    return [pl.BlockSpec(memory_space=pltpu.VMEM)] * count


LIMIT = pltpu.CompilerParams(vmem_limit_bytes=24 * 2**20)


def call(body, args, outs, cost, scratch=(), in_specs=None):
    return pl.pallas_call(
        body,
        out_shape=outs,
        in_specs=in_specs or vmem(len(args)),
        out_specs=vmem(len(outs)),
        scratch_shapes=scratch,
        compiler_params=LIMIT,
        cost_estimate=pl.CostEstimate(flops=cost, bytes_accessed=cost, transcendentals=0),
    )(*args)


def gathered(q, axis):
    def swap(value, apart):
        return lax.ppermute(value, axis, [(i, i ^ apart) for i in range(lax.axis_size(axis))])

    far = swap(q, 2)
    return q, swap(q, 1), far, swap(far, 1)


def rate_term(pieces, rate_blocks, pattern, bracket):
    cells, levels = pieces[0].shape
    return pl.pallas_call(
        functools.partial(rate_kernel, "lev"),
        in_specs=[pl.BlockSpec(memory_space=pltpu.SMEM)] + vmem(len(pieces) + 2),
        out_specs=pl.BlockSpec(memory_space=pltpu.VMEM),
        out_shape=jax.ShapeDtypeStruct((cells, levels), jnp.float32),
        scratch_shapes=[pltpu.VMEM((cells, len(pieces) * levels), jnp.bfloat16)],
        compiler_params=LIMIT,
        cost_estimate=pl.CostEstimate(
            flops=2 * cells * rate_blocks.size, bytes_accessed=2 * rate_blocks.size, transcendentals=0
        ),
    )(pattern, *pieces, rate_blocks, bracket)


def shifted(value, axis):
    peers = lax.axis_size(axis)
    return lax.ppermute(value, axis, [(i, i + 1) for i in range(peers - 1)])


def local(
    populations,
    rate_blocks,
    pattern,
    bracket,
    cross_section,
    emission,
    absorber,
    stream_speed,
    cross_speed,
    inflow,
):
    cells, levels = populations.shape
    strips = lax.axis_size("cell")
    bracket = bracket.reshape(1, cells)
    cross = cross_section.reshape(1, levels)
    crosses = cross_section.reshape(levels // LANES, LANES)
    emission = emission.reshape(1, levels)
    absorber = absorber.reshape(1, cells)
    stream = stream_speed.reshape(1, cells)
    crossways = cross_speed.reshape(1, cells)

    field = jax.ShapeDtypeStruct((cells, levels), jnp.float32)
    rounded = jax.ShapeDtypeStruct((cells, levels), jnp.bfloat16)
    layer = jax.ShapeDtypeStruct((NY, levels), jnp.bfloat16)
    tiles = jax.ShapeDtypeStruct((strips, ROWS, LANES), jnp.float32)
    size = cells * levels * 4

    def swap(value):
        return lax.all_to_all(value, "cell", 0, 0, tiled=True)

    sources = (populations, cross, emission, absorber)
    q, last, leaving = call(
        first_kernel,
        sources,
        (rounded, layer, jax.ShapeDtypeStruct((strips, 2 * ROWS, LANES), jnp.bfloat16)),
        3 * size,
        [pltpu.VMEM(value.shape, value.dtype) for value in sources]
        + [pltpu.SemaphoreType.DMA((len(sources),))],
        [pl.BlockSpec(memory_space=pltpu.HBM)] * len(sources),
    )
    pieces = gathered(q, "lev")
    arrived = shifted(last, "cell")
    sent = swap(leaving)
    entered, passes = call(
        functools.partial(first_scan_kernel, "cell"),
        (sent, crosses),
        (tiles, tiles),
        size,
        [pltpu.VMEM(tiles.shape, jnp.float32)],
    )
    rates = rate_term(pieces, rate_blocks, pattern, bracket)
    same, other = call(
        functools.partial(response_kernel, "cell", cells // NY),
        (sent, crosses, emission.reshape(crosses.shape)),
        (tiles, tiles),
        size,
    )
    part, leaving = call(
        functools.partial(step_kernel, False, "cell"),
        (populations, rates, entered, arrived, inflow, cross, emission, absorber, stream, crossways),
        (field, jax.ShapeDtypeStruct((strips, 2 * ROWS, LANES), jnp.float32)),
        5 * size,
    )
    swapped = swap(leaving)
    middle, q, last = call(
        middle_kernel, (part, swapped, cross, absorber), (field, rounded, layer), 3 * size
    )
    pieces = gathered(q, "lev")
    arrived = shifted(last, "cell")
    (entering,) = call(
        second_scan_kernel,
        (swapped, entered, passes, same, other),
        (tiles,),
        size,
        [pltpu.VMEM(tiles.shape, jnp.float32)],
    )
    entering = swap(entering)
    rates = rate_term(pieces, rate_blocks, pattern, bracket)
    return call(
        functools.partial(step_kernel, True, "cell"),
        (middle, rates, entering, arrived, inflow, cross, emission, absorber, stream, crossways, populations),
        (field, field),
        5 * size,
    )


def solution(mesh):
    in_specs = (
        P("cell", "lev"),
        P(None, "lev", None, None, None),
        P("lev", None),
        P("cell"),
        P("lev"),
        P("lev"),
        P("cell"),
        P("cell"),
        P("cell"),
        P(None, "lev"),
    )
    out_specs = (P("cell", "lev"), P("cell", "lev"))
    return jax.shard_map(local, mesh=mesh, in_specs=in_specs, out_specs=out_specs, check_vma=False)
```

```python
import functools

import jax
import jax.numpy as jnp
from jax import lax
from jax.experimental import pallas as pl
from jax.experimental.pallas import tpu as pltpu
from jax.sharding import PartitionSpec as P

NY = 16
LANES = 128
ROWS = 8
HALF = 4
PARTS = 2
FIRST = 63
time_step = 0.25


def column(row):
    n = row.shape[1]
    at_row = lax.broadcasted_iota(jnp.int32, (n, n), 0)
    at_column = lax.broadcasted_iota(jnp.int32, (n, n), 1)
    return jnp.sum(jnp.where(at_row == at_column, row, jnp.zeros_like(row)), axis=1, keepdims=True)


def layers(value):
    return [value[k : k + NY] for k in range(0, value.shape[0], NY)]


def exits(passed, emitted):
    down, up = emitted[0], emitted[-1]
    for t, e in zip(passed[1:], emitted[1:]):
        down = t * down + e
    for t, e in zip(passed[-2::-1], emitted[-2::-1]):
        up = t * up + e
    return down, up


def top(value):
    return lax.broadcasted_iota(jnp.int32, value.shape, 0) < HALF


def to_tiles(down, up):
    tiles = []
    for k in range(0, NY, ROWS):
        d, u = down[k : k + ROWS], up[k : k + ROWS]
        tiles.append(jnp.where(top(d), d, pltpu.roll(u, HALF, 0)))
        tiles.append(jnp.where(top(d), pltpu.roll(d, HALF, 0), u))
    return tiles


def from_tiles(tiles):
    down, up = [], []
    for first, second in zip(tiles[::2], tiles[1::2]):
        down.append(jnp.where(top(first), first, pltpu.roll(second, HALF, 0)))
        up.append(jnp.where(top(first), pltpu.roll(first, HALF, 0), second))
    return jnp.concatenate(down, axis=0), jnp.concatenate(up, axis=0)


def get_enters(enter_ref, group, groups):
    return from_tiles([enter_ref[k * groups + group, :ROWS] for k in range(NY // HALF)])


def depth_tiles(absorber):
    lane = lax.broadcasted_iota(jnp.int32, (NY, LANES), 1)
    by_layer = layers(absorber)
    count = len(by_layer)
    forward = reverse = jnp.zeros((NY, LANES), jnp.float32)
    for k, value in enumerate(by_layer):
        high = value.astype(jnp.bfloat16).astype(jnp.float32)
        for j, part in enumerate((high, value - high)):
            forward = jnp.where(lane == PARTS * k + j, part, forward)
            reverse = jnp.where(lane == PARTS * (count - 1 - k) + j, part, reverse)
    return to_tiles(forward, reverse)


def absorbed_of(passed, emitted, enter_down, enter_up):
    count = len(passed)
    downward, upward = [None] * count, [None] * count
    running = enter_down
    for k in range(count):
        running = emitted[k] if running is None else passed[k] * running + emitted[k]
        downward[k] = running
    running = enter_up
    for k in reversed(range(count)):
        running = emitted[k] if running is None else passed[k] * running + emitted[k]
        upward[k] = running
    return [
        (1.0 - t) * (d + u - 2.0 * e) for t, d, u, e in zip(passed, downward, upward, emitted)
    ]


def advection(layered, boundary, along_x, forward_y, backward_y):
    result, upstream = [], boundary
    for k, here in enumerate(layered):
        before = pltpu.roll(here, 1, 0)
        after = pltpu.roll(here, NY - 1, 0)
        result.append(
            -along_x[k] * (here - upstream) - forward_y[k] * (here - before) - backward_y[k] * (after - here)
        )
        upstream = here
    return result


def depth_lanes(count):
    return lax.broadcasted_iota(jnp.int32, (ROWS, LANES), 1) < PARTS * count


def first_kernel(p_hbm, cross_hbm, emission_hbm, absorber_hbm, q_ref, last_ref, exit_ref, *scratch):
    sems = scratch[-1]
    copies = [
        pltpu.make_async_copy(source, target, sems.at[i])
        for i, (source, target) in enumerate(
            zip((p_hbm, cross_hbm, emission_hbm, absorber_hbm), scratch[:-1])
        )
    ]
    for copy in copies:
        copy.start()
    for copy in copies:
        copy.wait()
    p_ref, cross_ref, emission_ref, absorber_ref = scratch[:-1]
    absorber = column(absorber_ref[...])
    depths = depth_tiles(absorber)
    groups = p_ref.shape[1] // LANES
    for g in range(groups):
        at = slice(g * LANES, (g + 1) * LANES)
        p = p_ref[:, at]
        q = p.astype(jnp.bfloat16)
        q_ref[:, at] = q
        last_ref[:, at] = q[-NY:]
        passed = layers(jnp.exp(-(absorber * cross_ref[:, at])))
        emitted = layers(p * emission_ref[:, at])
        for k, (tile, depth) in enumerate(zip(to_tiles(*exits(passed, emitted)), depths)):
            rest = tile - tile.astype(jnp.bfloat16).astype(jnp.float32)
            below = jnp.where(depth_lanes(len(passed)), depth, rest)
            exit_ref[k * groups + g] = jnp.concatenate([tile, below], axis=0).astype(jnp.bfloat16)


def scan(exit_of, pass_ref, enter_ref):
    count = enter_ref.shape[0]
    carry = jnp.zeros(enter_ref.shape[1:], jnp.float32)
    upper = top(carry)
    for i in range(count):
        j = count - 1 - i
        enter_ref[i, :HALF] = carry[:HALF]
        enter_ref[j, HALF:] = carry[HALF:]
        carry = jnp.where(upper, pass_ref[i], pass_ref[j]) * carry + jnp.where(
            upper, exit_of(i), exit_of(j)
        )


def first_scan_kernel(axis, count, arrived_ref, cross_ref, enter_ref, pass_ref, exit_ref):
    group = lax.rem(lax.axis_index(axis), cross_ref.shape[0])
    cross = cross_ref[pl.ds(group, 1), :]
    for s in range(arrived_ref.shape[0]):
        arrived = arrived_ref[s].astype(jnp.float32)
        depths = depth_lanes(count)
        exit_ref[s] = arrived[:ROWS] + jnp.where(depths, 0.0, arrived[ROWS:])
        depth = jnp.sum(jnp.where(depths, arrived[ROWS:], 0.0), axis=1, keepdims=True)
        pass_ref[s] = jnp.exp(-(depth * cross))
    scan(lambda at: exit_ref[at], pass_ref, enter_ref)


def response_kernel(axis, count, arrived_ref, cross_ref, emission_ref, same_ref, other_ref):
    group = lax.rem(lax.axis_index(axis), cross_ref.shape[0])
    cross = cross_ref[pl.ds(group, 1), :]
    emission = time_step * emission_ref[pl.ds(group, 1), :]
    lane = lax.broadcasted_iota(jnp.int32, (ROWS, LANES), 1)
    mine = [(lane >= PARTS * k) & (lane < PARTS * (k + 1)) for k in range(count)]
    for s in range(arrived_ref.shape[0]):
        depths = arrived_ref[s].astype(jnp.float32)[ROWS:]
        after = jnp.ones((ROWS, LANES), jnp.float32)
        taken = other = jnp.zeros((ROWS, LANES), jnp.float32)
        for k in reversed(range(count)):
            depth = jnp.sum(jnp.where(mine[k], depths, 0.0), axis=1, keepdims=True)
            t = jnp.exp(-(depth * cross))
            taken = taken + (1.0 - t)
            other = other + (after * after) * (t * (1.0 - t))
            after = after * t
        same_ref[s] = emission * (after * taken)
        other_ref[s] = emission * other


def second_scan_kernel(arrived_ref, entered_ref, pass_ref, same_ref, other_ref, enter_ref, exit_ref):
    for s in range(arrived_ref.shape[0]):
        entered = entered_ref[s]
        exit_ref[s] = (
            arrived_ref[s, ROWS:]
            + same_ref[s] * entered
            + other_ref[s] * pltpu.roll(entered, HALF, 0)
        )
    scan(lambda at: exit_ref[at], pass_ref, enter_ref)


def rate_kernel(axis, pattern_ref, *refs):
    pieces, (table_ref, bracket_ref, out_ref, q_ref) = refs[:-4], refs[-4:]
    brackets, rows, count = table_ref.shape[:3]
    width = pieces[0].shape[1]
    for place, piece in enumerate(pieces):
        q_ref[:, place * width : (place + 1) * width] = piece[...]
    me = lax.axis_index(axis)
    bracket = column(bracket_ref[...])

    def block(r, k):
        source = pattern_ref[r, k]
        place = lax.rem(source, rows) + rows * ((source // rows) ^ me)
        return q_ref[:, pl.ds(pl.multiple_of(place * LANES, LANES), LANES)]

    for r in range(rows):
        picked = jnp.concatenate([block(r, k) for k in range(count)], axis=1)
        both = jnp.concatenate(
            [
                jnp.concatenate([table_ref[b, r, k] for k in range(count)], axis=1)
                for b in range(brackets)
            ],
            axis=0,
        )
        product = lax.dot_general(
            picked, both, (((1,), (1,)), ((), ())), preferred_element_type=jnp.float32
        )
        out_ref[:, r * LANES : (r + 1) * LANES] = jnp.where(
            bracket == 0, product[:, :LANES], product[:, LANES:]
        )


def step_kernel(final, axis, *refs):
    (p_ref, rate_ref, enter_ref, arrived_ref, inflow_ref, cross_ref, emission_ref,
     absorber_ref, stream_ref, crossways_ref) = refs[:10]
    absorber = column(absorber_ref[...])
    along_x = layers(column(stream_ref[...]))
    along_y = column(crossways_ref[...])
    forward_y = layers(jnp.maximum(along_y, 0.0))
    backward_y = layers(jnp.minimum(along_y, 0.0))
    inlet = lax.axis_index(axis) == 0
    groups = p_ref.shape[1] // LANES
    for g in range(groups):
        at = slice(g * LANES, (g + 1) * LANES)
        p = layers(p_ref[:, at])
        emission = emission_ref[:, at]
        emitted = [value * emission for value in p]
        passed = layers(jnp.exp(-(absorber * cross_ref[:, at])))
        entering = get_enters(enter_ref, g, groups) if final else (None, None)
        absorbed = absorbed_of(passed, emitted, *entering)
        boundary = jnp.where(inlet, inflow_ref[:, at], arrived_ref[:, at].astype(jnp.float32))
        carried = advection(p, boundary, along_x, forward_y, backward_y)
        rates = layers(rate_ref[:, at])
        tendency = [q - e + a + v for q, e, a, v in zip(rates, emitted, absorbed, carried)]
        if final:
            start_ref, updated_ref, absorption_ref = refs[10:]
            start = layers(start_ref[:, at])
            for k, rate in enumerate(tendency):
                here = slice(k * NY, (k + 1) * NY)
                updated_ref[here, at] = 0.5 * (start[k] + p[k] + time_step * rate)
                absorption_ref[here, at] = absorbed[k]
        else:
            middle_ref, swap_ref = refs[10:]
            middle = [value + time_step * rate for value, rate in zip(p, tendency)]
            for k, value in enumerate(middle):
                middle_ref[k * NY : (k + 1) * NY, at] = value
            leaving = to_tiles(*exits(passed, [value * emission for value in middle]))
            for k, tile in enumerate(leaving):
                swap_ref[k * groups + g, :ROWS] = enter_ref[k * groups + g]
                swap_ref[k * groups + g, ROWS:] = tile


def middle_kernel(part_ref, swap_ref, cross_ref, absorber_ref, middle_ref, q_ref, last_ref):
    absorber = column(absorber_ref[...])
    groups = part_ref.shape[1] // LANES
    for g in range(groups):
        at = slice(g * LANES, (g + 1) * LANES)
        part = layers(part_ref[:, at])
        passed = layers(jnp.exp(-(absorber * cross_ref[:, at])))
        downward, upward = get_enters(swap_ref, g, groups)
        count = len(passed)
        down, up = [None] * count, [None] * count
        for k in range(count):
            downward = passed[k] * downward
            down[k] = downward
        for k in reversed(range(count)):
            upward = passed[k] * upward
            up[k] = upward
        for k in range(count):
            here = slice(k * NY, (k + 1) * NY)
            value = part[k] + time_step * ((1.0 - passed[k]) * (down[k] + up[k]))
            middle_ref[here, at] = value
            q_ref[here, at] = value.astype(jnp.bfloat16)
            if k == count - 1:
                last_ref[:, at] = value.astype(jnp.bfloat16)


def vmem(count):
    return [pl.BlockSpec(memory_space=pltpu.VMEM)] * count


LIMIT = pltpu.CompilerParams(vmem_limit_bytes=24 * 2**20)


def call(body, args, outs, cost, scratch=(), in_specs=None, params=LIMIT):
    return pl.pallas_call(
        body,
        out_shape=outs,
        in_specs=in_specs or vmem(len(args)),
        out_specs=vmem(len(outs)),
        scratch_shapes=scratch,
        compiler_params=params,
        cost_estimate=pl.CostEstimate(flops=cost, bytes_accessed=cost, transcendentals=0),
    )(*args)


def gathered(q, axis):
    def swap(value, apart):
        return lax.ppermute(value, axis, [(i, i ^ apart) for i in range(lax.axis_size(axis))])

    far = swap(q, 2)
    return q, swap(q, 1), far, swap(far, 1)


def rate_term(pieces, rate_blocks, pattern, bracket):
    cells, levels = pieces[0].shape
    return pl.pallas_call(
        functools.partial(rate_kernel, "lev"),
        in_specs=[pl.BlockSpec(memory_space=pltpu.SMEM)] + vmem(len(pieces) + 2),
        out_specs=pl.BlockSpec(memory_space=pltpu.VMEM),
        out_shape=jax.ShapeDtypeStruct((cells, levels), jnp.float32),
        scratch_shapes=[pltpu.VMEM((cells, len(pieces) * levels), jnp.bfloat16)],
        compiler_params=LIMIT,
        cost_estimate=pl.CostEstimate(
            flops=2 * cells * rate_blocks.size, bytes_accessed=2 * rate_blocks.size, transcendentals=0
        ),
    )(pattern, *pieces, rate_blocks, bracket)


def shifted(value, axis):
    peers = lax.axis_size(axis)
    return lax.ppermute(value, axis, [(i, i + 1) for i in range(peers - 1)])


def local(
    populations,
    rate_blocks,
    pattern,
    bracket,
    cross_section,
    emission,
    absorber,
    stream_speed,
    cross_speed,
    inflow,
):
    cells, levels = populations.shape
    strips = lax.axis_size("cell")
    bracket = bracket.reshape(1, cells)
    cross = cross_section.reshape(1, levels)
    crosses = cross_section.reshape(levels // LANES, LANES)
    emission = emission.reshape(1, levels)
    absorber = absorber.reshape(1, cells)
    stream = stream_speed.reshape(1, cells)
    crossways = cross_speed.reshape(1, cells)

    field = jax.ShapeDtypeStruct((cells, levels), jnp.float32)
    rounded = jax.ShapeDtypeStruct((cells, levels), jnp.bfloat16)
    layer = jax.ShapeDtypeStruct((NY, levels), jnp.bfloat16)
    tiles = jax.ShapeDtypeStruct((strips, ROWS, LANES), jnp.float32)
    size = cells * levels * 4

    def swap(value):
        return lax.all_to_all(value, "cell", 0, 0, tiled=True)

    sources = (populations, cross, emission, absorber)
    q, last, leaving = call(
        first_kernel,
        sources,
        (rounded, layer, jax.ShapeDtypeStruct((strips, 2 * ROWS, LANES), jnp.bfloat16)),
        3 * size,
        [pltpu.VMEM(value.shape, value.dtype) for value in sources]
        + [pltpu.SemaphoreType.DMA((len(sources),))],
        [pl.BlockSpec(memory_space=pl.ANY)] * len(sources),
        pltpu.CompilerParams(vmem_limit_bytes=FIRST * 2**20),
    )
    pieces = gathered(q, "lev")
    arrived = shifted(last, "cell")
    sent, rates = lax.optimization_barrier(
        (swap(leaving), rate_term(pieces, rate_blocks, pattern, bracket))
    )
    entered, passes = call(
        functools.partial(first_scan_kernel, "cell", cells // NY),
        (sent, crosses),
        (tiles, tiles),
        size,
        [pltpu.VMEM(tiles.shape, jnp.float32)],
    )
    same, other = call(
        functools.partial(response_kernel, "cell", cells // NY),
        (sent, crosses, emission.reshape(crosses.shape)),
        (tiles, tiles),
        size,
    )
    part, leaving = call(
        functools.partial(step_kernel, False, "cell"),
        (populations, rates, entered, arrived, inflow, cross, emission, absorber, stream, crossways),
        (field, jax.ShapeDtypeStruct((strips, 2 * ROWS, LANES), jnp.float32)),
        5 * size,
    )
    swapped = swap(leaving)
    middle, q, last = call(
        middle_kernel, (part, swapped, cross, absorber), (field, rounded, layer), 3 * size
    )
    pieces = gathered(q, "lev")
    arrived = shifted(last, "cell")
    (entering,) = call(
        second_scan_kernel,
        (swapped, entered, passes, same, other),
        (tiles,),
        size,
        [pltpu.VMEM(tiles.shape, jnp.float32)],
    )
    entering = swap(entering)
    rates = rate_term(pieces, rate_blocks, pattern, bracket)
    return call(
        functools.partial(step_kernel, True, "cell"),
        (middle, rates, entering, arrived, inflow, cross, emission, absorber, stream, crossways, populations),
        (field, field),
        5 * size,
    )


def solution(mesh):
    in_specs = (
        P("cell", "lev"),
        P(None, "lev", None, None, None),
        P("lev", None),
        P("cell"),
        P("lev"),
        P("lev"),
        P("cell"),
        P("cell"),
        P("cell"),
        P(None, "lev"),
    )
    out_specs = (P("cell", "lev"), P("cell", "lev"))
    return jax.shard_map(local, mesh=mesh, in_specs=in_specs, out_specs=out_specs, check_vma=False)
```

```python
import functools

import jax
import jax.numpy as jnp
from jax import lax
from jax.experimental import pallas as pl
from jax.experimental.pallas import tpu as pltpu
from jax.sharding import PartitionSpec as P

NY = 16
LANES = 128
ROWS = 8
HALF = 4
PARTS = 2
FIRST = 53
LONG = 40000
time_step = 0.25


def column(row):
    n = row.shape[1]
    at_row = lax.broadcasted_iota(jnp.int32, (n, n), 0)
    at_column = lax.broadcasted_iota(jnp.int32, (n, n), 1)
    return jnp.sum(jnp.where(at_row == at_column, row, jnp.zeros_like(row)), axis=1, keepdims=True)


def layers(value):
    return [value[k : k + NY] for k in range(0, value.shape[0], NY)]


def exits(passed, emitted):
    down, up = emitted[0], emitted[-1]
    for t, e in zip(passed[1:], emitted[1:]):
        down = t * down + e
    for t, e in zip(passed[-2::-1], emitted[-2::-1]):
        up = t * up + e
    return down, up


def top(value):
    return lax.broadcasted_iota(jnp.int32, value.shape, 0) < HALF


def to_tiles(down, up):
    tiles = []
    for k in range(0, NY, ROWS):
        d, u = down[k : k + ROWS], up[k : k + ROWS]
        tiles.append(jnp.where(top(d), d, pltpu.roll(u, HALF, 0)))
        tiles.append(jnp.where(top(d), pltpu.roll(d, HALF, 0), u))
    return tiles


def from_tiles(tiles):
    down, up = [], []
    for first, second in zip(tiles[::2], tiles[1::2]):
        down.append(jnp.where(top(first), first, pltpu.roll(second, HALF, 0)))
        up.append(jnp.where(top(first), pltpu.roll(first, HALF, 0), second))
    return jnp.concatenate(down, axis=0), jnp.concatenate(up, axis=0)


def get_enters(enter_ref, group, groups):
    return from_tiles([enter_ref[k * groups + group, :ROWS] for k in range(NY // HALF)])


def depth_tiles(absorber):
    lane = lax.broadcasted_iota(jnp.int32, (NY, LANES), 1)
    by_layer = layers(absorber)
    count = len(by_layer)
    forward = reverse = jnp.zeros((NY, LANES), jnp.float32)
    for k, value in enumerate(by_layer):
        high = value.astype(jnp.bfloat16).astype(jnp.float32)
        for j, part in enumerate((high, value - high)):
            forward = jnp.where(lane == PARTS * k + j, part, forward)
            reverse = jnp.where(lane == PARTS * (count - 1 - k) + j, part, reverse)
    return to_tiles(forward, reverse)


def absorbed_of(passed, emitted, enter_down, enter_up):
    count = len(passed)
    downward, upward = [None] * count, [None] * count
    running = enter_down
    for k in range(count):
        running = emitted[k] if running is None else passed[k] * running + emitted[k]
        downward[k] = running
    running = enter_up
    for k in reversed(range(count)):
        running = emitted[k] if running is None else passed[k] * running + emitted[k]
        upward[k] = running
    return [
        (1.0 - t) * (d + u - 2.0 * e) for t, d, u, e in zip(passed, downward, upward, emitted)
    ]


def advection(layered, boundary, along_x, forward_y, backward_y):
    result, upstream = [], boundary
    for k, here in enumerate(layered):
        before = pltpu.roll(here, 1, 0)
        after = pltpu.roll(here, NY - 1, 0)
        result.append(
            -along_x[k] * (here - upstream) - forward_y[k] * (here - before) - backward_y[k] * (after - here)
        )
        upstream = here
    return result


def depth_lanes(count):
    return lax.broadcasted_iota(jnp.int32, (ROWS, LANES), 1) < PARTS * count


def first_kernel(p_hbm, cross_hbm, emission_hbm, absorber_hbm, q_ref, last_ref, exit_ref, *scratch):
    sems = scratch[-1]
    copies = [
        pltpu.make_async_copy(source, target, sems.at[i])
        for i, (source, target) in enumerate(
            zip((p_hbm, cross_hbm, emission_hbm, absorber_hbm), scratch[:-1])
        )
    ]
    for copy in copies:
        copy.start()
    for copy in copies:
        copy.wait()
    p_ref, cross_ref, emission_ref, absorber_ref = scratch[:-1]
    absorber = column(absorber_ref[...])
    depths = depth_tiles(absorber)
    groups = p_ref.shape[1] // LANES
    for g in range(groups):
        at = slice(g * LANES, (g + 1) * LANES)
        p = p_ref[:, at]
        q = p.astype(jnp.bfloat16)
        q_ref[:, at] = q
        last_ref[:, at] = q[-NY:]
        passed = layers(jnp.exp(-(absorber * cross_ref[:, at])))
        emitted = layers(p * emission_ref[:, at])
        for k, (tile, depth) in enumerate(zip(to_tiles(*exits(passed, emitted)), depths)):
            rest = tile - tile.astype(jnp.bfloat16).astype(jnp.float32)
            below = jnp.where(depth_lanes(len(passed)), depth, rest)
            exit_ref[k * groups + g] = jnp.concatenate([tile, below], axis=0).astype(jnp.bfloat16)


def scan(exit_of, pass_ref, enter_ref):
    count = enter_ref.shape[0]
    carry = jnp.zeros(enter_ref.shape[1:], jnp.float32)
    upper = top(carry)
    for i in range(count):
        j = count - 1 - i
        enter_ref[i, :HALF] = carry[:HALF]
        enter_ref[j, HALF:] = carry[HALF:]
        carry = jnp.where(upper, pass_ref[i], pass_ref[j]) * carry + jnp.where(
            upper, exit_of(i), exit_of(j)
        )


def first_scan_kernel(axis, count, arrived_ref, cross_ref, enter_ref, pass_ref, exit_ref):
    group = lax.rem(lax.axis_index(axis), cross_ref.shape[0])
    cross = cross_ref[pl.ds(group, 1), :]
    for s in range(arrived_ref.shape[0]):
        arrived = arrived_ref[s].astype(jnp.float32)
        depths = depth_lanes(count)
        exit_ref[s] = arrived[:ROWS] + jnp.where(depths, 0.0, arrived[ROWS:])
        depth = jnp.sum(jnp.where(depths, arrived[ROWS:], 0.0), axis=1, keepdims=True)
        pass_ref[s] = jnp.exp(-(depth * cross))
    scan(lambda at: exit_ref[at], pass_ref, enter_ref)


def response_kernel(axis, count, arrived_ref, cross_ref, emission_ref, same_ref, other_ref):
    group = lax.rem(lax.axis_index(axis), cross_ref.shape[0])
    cross = cross_ref[pl.ds(group, 1), :]
    emission = time_step * emission_ref[pl.ds(group, 1), :]
    lane = lax.broadcasted_iota(jnp.int32, (ROWS, LANES), 1)
    mine = [(lane >= PARTS * k) & (lane < PARTS * (k + 1)) for k in range(count)]
    for s in range(arrived_ref.shape[0]):
        depths = arrived_ref[s].astype(jnp.float32)[ROWS:]
        after = jnp.ones((ROWS, LANES), jnp.float32)
        taken = other = jnp.zeros((ROWS, LANES), jnp.float32)
        for k in reversed(range(count)):
            depth = jnp.sum(jnp.where(mine[k], depths, 0.0), axis=1, keepdims=True)
            t = jnp.exp(-(depth * cross))
            taken = taken + (1.0 - t)
            other = other + (after * after) * (t * (1.0 - t))
            after = after * t
        same_ref[s] = emission * (after * taken)
        other_ref[s] = emission * other


def second_scan_kernel(arrived_ref, entered_ref, pass_ref, same_ref, other_ref, enter_ref, exit_ref):
    for s in range(arrived_ref.shape[0]):
        entered = entered_ref[s]
        exit_ref[s] = (
            arrived_ref[s, ROWS:]
            + same_ref[s] * entered
            + other_ref[s] * pltpu.roll(entered, HALF, 0)
        )
    scan(lambda at: exit_ref[at], pass_ref, enter_ref)


def rate_kernel(axis, pattern_ref, *refs):
    pieces, (table_ref, bracket_ref, out_ref, q_ref) = refs[:-4], refs[-4:]
    brackets, rows, count = table_ref.shape[:3]
    width = pieces[0].shape[1]
    for place, piece in enumerate(pieces):
        q_ref[:, place * width : (place + 1) * width] = piece[...]
    me = lax.axis_index(axis)
    bracket = column(bracket_ref[...])

    def block(r, k):
        source = pattern_ref[k, r]
        place = lax.rem(source, rows) + rows * ((source // rows) ^ me)
        return q_ref[:, pl.ds(pl.multiple_of(place * LANES, LANES), LANES)]

    for r in range(rows):
        picked = jnp.concatenate([block(r, k) for k in range(count)], axis=1)
        both = jnp.concatenate(
            [
                jnp.concatenate([table_ref[b, r, k] for k in range(count)], axis=1)
                for b in range(brackets)
            ],
            axis=0,
        )
        product = lax.dot_general(
            picked, both, (((1,), (1,)), ((), ())), preferred_element_type=jnp.float32
        )
        out_ref[:, r * LANES : (r + 1) * LANES] = jnp.where(
            bracket == 0, product[:, :LANES], product[:, LANES:]
        )


def step_kernel(final, axis, *refs):
    (p_ref, rate_ref, enter_ref, arrived_ref, inflow_ref, cross_ref, emission_ref,
     absorber_ref, stream_ref, crossways_ref) = refs[:10]
    absorber = column(absorber_ref[...])
    along_x = layers(column(stream_ref[...]))
    along_y = column(crossways_ref[...])
    forward_y = layers(jnp.maximum(along_y, 0.0))
    backward_y = layers(jnp.minimum(along_y, 0.0))
    inlet = lax.axis_index(axis) == 0
    groups = p_ref.shape[1] // LANES
    for g in range(groups):
        at = slice(g * LANES, (g + 1) * LANES)
        p = layers(p_ref[:, at])
        emission = emission_ref[:, at]
        emitted = [value * emission for value in p]
        passed = layers(jnp.exp(-(absorber * cross_ref[:, at])))
        entering = get_enters(enter_ref, g, groups) if final else (None, None)
        absorbed = absorbed_of(passed, emitted, *entering)
        boundary = jnp.where(inlet, inflow_ref[:, at], arrived_ref[:, at].astype(jnp.float32))
        carried = advection(p, boundary, along_x, forward_y, backward_y)
        rates = layers(rate_ref[:, at])
        tendency = [q - e + a + v for q, e, a, v in zip(rates, emitted, absorbed, carried)]
        if final:
            start_ref, updated_ref, absorption_ref = refs[10:]
            start = layers(start_ref[:, at])
            for k, rate in enumerate(tendency):
                here = slice(k * NY, (k + 1) * NY)
                updated_ref[here, at] = 0.5 * (start[k] + p[k] + time_step * rate)
                absorption_ref[here, at] = absorbed[k]
        else:
            middle_ref, swap_ref = refs[10:]
            middle = [value + time_step * rate for value, rate in zip(p, tendency)]
            for k, value in enumerate(middle):
                middle_ref[k * NY : (k + 1) * NY, at] = value
            leaving = to_tiles(*exits(passed, [value * emission for value in middle]))
            for k, tile in enumerate(leaving):
                swap_ref[k * groups + g, :ROWS] = enter_ref[k * groups + g]
                swap_ref[k * groups + g, ROWS:] = tile


def middle_kernel(part_ref, swap_ref, cross_ref, absorber_ref, middle_ref, q_ref, last_ref):
    absorber = column(absorber_ref[...])
    groups = part_ref.shape[1] // LANES
    for g in range(groups):
        at = slice(g * LANES, (g + 1) * LANES)
        part = layers(part_ref[:, at])
        passed = layers(jnp.exp(-(absorber * cross_ref[:, at])))
        downward, upward = get_enters(swap_ref, g, groups)
        count = len(passed)
        down, up = [None] * count, [None] * count
        for k in range(count):
            downward = passed[k] * downward
            down[k] = downward
        for k in reversed(range(count)):
            upward = passed[k] * upward
            up[k] = upward
        for k in range(count):
            here = slice(k * NY, (k + 1) * NY)
            value = part[k] + time_step * ((1.0 - passed[k]) * (down[k] + up[k]))
            middle_ref[here, at] = value
            q_ref[here, at] = value.astype(jnp.bfloat16)
            if k == count - 1:
                last_ref[:, at] = value.astype(jnp.bfloat16)


def vmem(count):
    return [pl.BlockSpec(memory_space=pltpu.VMEM)] * count


LIMIT = pltpu.CompilerParams(vmem_limit_bytes=24 * 2**20)


def call(body, args, outs, cost, scratch=(), in_specs=None, params=LIMIT):
    return pl.pallas_call(
        body,
        out_shape=outs,
        in_specs=in_specs or vmem(len(args)),
        out_specs=vmem(len(outs)),
        scratch_shapes=scratch,
        compiler_params=params,
        cost_estimate=pl.CostEstimate(flops=cost, bytes_accessed=cost, transcendentals=0),
    )(*args)


def gathered(q, axis):
    def swap(value, apart):
        return lax.ppermute(value, axis, [(i, i ^ apart) for i in range(lax.axis_size(axis))])

    far = swap(q, 2)
    return q, swap(q, 1), far, swap(far, 1)


def rate_term(pieces, rate_blocks, pattern, bracket):
    cells, levels = pieces[0].shape
    return pl.pallas_call(
        functools.partial(rate_kernel, "lev"),
        in_specs=[pl.BlockSpec(memory_space=pltpu.SMEM)] + vmem(len(pieces) + 2),
        out_specs=pl.BlockSpec(memory_space=pltpu.VMEM),
        out_shape=jax.ShapeDtypeStruct((cells, levels), jnp.float32),
        scratch_shapes=[pltpu.VMEM((cells, len(pieces) * levels), jnp.bfloat16)],
        compiler_params=LIMIT,
        cost_estimate=pl.CostEstimate(
            flops=2 * cells * rate_blocks.size, bytes_accessed=2 * rate_blocks.size, transcendentals=0
        ),
    )(pattern, *pieces, rate_blocks, bracket)


def shifted(value, axis):
    peers = lax.axis_size(axis)
    return lax.ppermute(value, axis, [(i, i + 1) for i in range(peers - 1)])


def local(
    populations,
    rate_blocks,
    pattern,
    bracket,
    cross_section,
    emission,
    absorber,
    stream_speed,
    cross_speed,
    inflow,
):
    cells, levels = populations.shape
    strips = lax.axis_size("cell")
    bracket = bracket.reshape(1, cells)
    pattern = pattern.T
    cross = cross_section.reshape(1, levels)
    crosses = cross_section.reshape(levels // LANES, LANES)
    emission = emission.reshape(1, levels)
    absorber = absorber.reshape(1, cells)
    stream = stream_speed.reshape(1, cells)
    crossways = cross_speed.reshape(1, cells)

    field = jax.ShapeDtypeStruct((cells, levels), jnp.float32)
    rounded = jax.ShapeDtypeStruct((cells, levels), jnp.bfloat16)
    layer = jax.ShapeDtypeStruct((NY, levels), jnp.bfloat16)
    tiles = jax.ShapeDtypeStruct((strips, ROWS, LANES), jnp.float32)
    size = cells * levels * 4

    def swap(value):
        return lax.all_to_all(value, "cell", 0, 0, tiled=True)

    sources = (populations, cross, emission, absorber)
    q, last, leaving = call(
        first_kernel,
        sources,
        (rounded, layer, jax.ShapeDtypeStruct((strips, 2 * ROWS, LANES), jnp.bfloat16)),
        LONG * size,
        [pltpu.VMEM(value.shape, value.dtype) for value in sources]
        + [pltpu.SemaphoreType.DMA((len(sources),))],
        [pl.BlockSpec(memory_space=pl.ANY)] * len(sources),
        pltpu.CompilerParams(vmem_limit_bytes=FIRST * 2**20),
    )
    pieces = gathered(q, "lev")
    arrived = shifted(last, "cell")
    sent, rates = lax.optimization_barrier(
        (swap(leaving), rate_term(pieces, rate_blocks, pattern, bracket))
    )
    entered, passes = call(
        functools.partial(first_scan_kernel, "cell", cells // NY),
        (sent, crosses),
        (tiles, tiles),
        size,
        [pltpu.VMEM(tiles.shape, jnp.float32)],
    )
    same, other = call(
        functools.partial(response_kernel, "cell", cells // NY),
        (sent, crosses, emission.reshape(crosses.shape)),
        (tiles, tiles),
        size,
    )
    part, leaving = call(
        functools.partial(step_kernel, False, "cell"),
        (populations, rates, entered, arrived, inflow, cross, emission, absorber, stream, crossways),
        (field, jax.ShapeDtypeStruct((strips, 2 * ROWS, LANES), jnp.float32)),
        5 * size,
    )
    swapped = swap(leaving)
    middle, q, last = call(
        middle_kernel, (part, swapped, cross, absorber), (field, rounded, layer), 3 * size
    )
    pieces = gathered(q, "lev")
    arrived = shifted(last, "cell")
    (entering,) = call(
        second_scan_kernel,
        (swapped, entered, passes, same, other),
        (tiles,),
        size,
        [pltpu.VMEM(tiles.shape, jnp.float32)],
    )
    entering = swap(entering)
    rates = rate_term(pieces, rate_blocks, pattern, bracket)
    return call(
        functools.partial(step_kernel, True, "cell"),
        (middle, rates, entering, arrived, inflow, cross, emission, absorber, stream, crossways, populations),
        (field, field),
        5 * size,
    )


def solution(mesh):
    in_specs = (
        P("cell", "lev"),
        P(None, "lev", None, None, None),
        P("lev", None),
        P("cell"),
        P("lev"),
        P("lev"),
        P("cell"),
        P("cell"),
        P("cell"),
        P(None, "lev"),
    )
    out_specs = (P("cell", "lev"), P("cell", "lev"))
    return jax.shard_map(local, mesh=mesh, in_specs=in_specs, out_specs=out_specs, check_vma=False)
```

```python
import functools

import jax
import jax.numpy as jnp
from jax import lax
from jax.experimental import pallas as pl
from jax.experimental.pallas import tpu as pltpu
from jax.sharding import PartitionSpec as P

NY = 16
LANES = 128
ROWS = 8
HALF = 4
PARTS = 2
FIRST = 57
LONG = 40000
time_step = 0.25


def column(row):
    n = row.shape[1]
    at_row = lax.broadcasted_iota(jnp.int32, (n, n), 0)
    at_column = lax.broadcasted_iota(jnp.int32, (n, n), 1)
    return jnp.sum(jnp.where(at_row == at_column, row, jnp.zeros_like(row)), axis=1, keepdims=True)


def layers(value):
    return [value[k : k + NY] for k in range(0, value.shape[0], NY)]


def exits(passed, emitted):
    down, up = emitted[0], emitted[-1]
    for t, e in zip(passed[1:], emitted[1:]):
        down = t * down + e
    for t, e in zip(passed[-2::-1], emitted[-2::-1]):
        up = t * up + e
    return down, up


def top(value):
    return lax.broadcasted_iota(jnp.int32, value.shape, 0) < HALF


def to_tiles(down, up):
    tiles = []
    for k in range(0, NY, ROWS):
        d, u = down[k : k + ROWS], up[k : k + ROWS]
        tiles.append(jnp.where(top(d), d, pltpu.roll(u, HALF, 0)))
        tiles.append(jnp.where(top(d), pltpu.roll(d, HALF, 0), u))
    return tiles


def from_tiles(tiles):
    down, up = [], []
    for first, second in zip(tiles[::2], tiles[1::2]):
        down.append(jnp.where(top(first), first, pltpu.roll(second, HALF, 0)))
        up.append(jnp.where(top(first), pltpu.roll(first, HALF, 0), second))
    return jnp.concatenate(down, axis=0), jnp.concatenate(up, axis=0)


def get_enters(enter_ref, group, groups):
    return from_tiles([enter_ref[k * groups + group, :ROWS] for k in range(NY // HALF)])


def depth_tiles(absorber):
    lane = lax.broadcasted_iota(jnp.int32, (NY, LANES), 1)
    by_layer = layers(absorber)
    count = len(by_layer)
    forward = reverse = jnp.zeros((NY, LANES), jnp.float32)
    for k, value in enumerate(by_layer):
        high = value.astype(jnp.bfloat16).astype(jnp.float32)
        for j, part in enumerate((high, value - high)):
            forward = jnp.where(lane == PARTS * k + j, part, forward)
            reverse = jnp.where(lane == PARTS * (count - 1 - k) + j, part, reverse)
    return to_tiles(forward, reverse)


def absorbed_of(passed, emitted, enter_down, enter_up):
    count = len(passed)
    downward, upward = [None] * count, [None] * count
    running = enter_down
    for k in range(count):
        running = emitted[k] if running is None else passed[k] * running + emitted[k]
        downward[k] = running
    running = enter_up
    for k in reversed(range(count)):
        running = emitted[k] if running is None else passed[k] * running + emitted[k]
        upward[k] = running
    return [
        (1.0 - t) * (d + u - 2.0 * e) for t, d, u, e in zip(passed, downward, upward, emitted)
    ]


def advection(layered, boundary, along_x, forward_y, backward_y):
    result, upstream = [], boundary
    for k, here in enumerate(layered):
        before = pltpu.roll(here, 1, 0)
        after = pltpu.roll(here, NY - 1, 0)
        result.append(
            -along_x[k] * (here - upstream) - forward_y[k] * (here - before) - backward_y[k] * (after - here)
        )
        upstream = here
    return result


def depth_lanes(count):
    return lax.broadcasted_iota(jnp.int32, (ROWS, LANES), 1) < PARTS * count


def first_kernel(p_hbm, cross_hbm, emission_hbm, absorber_hbm, q_ref, last_ref, exit_ref, *scratch):
    sems = scratch[-1]
    copies = [
        pltpu.make_async_copy(source, target, sems.at[i])
        for i, (source, target) in enumerate(
            zip((p_hbm, cross_hbm, emission_hbm, absorber_hbm), scratch[:-1])
        )
    ]
    for copy in copies:
        copy.start()
    for copy in copies:
        copy.wait()
    p_ref, cross_ref, emission_ref, absorber_ref = scratch[:-1]
    absorber = column(absorber_ref[...])
    depths = depth_tiles(absorber)
    groups = p_ref.shape[1] // LANES
    for g in range(groups):
        at = slice(g * LANES, (g + 1) * LANES)
        p = p_ref[:, at]
        q = p.astype(jnp.bfloat16)
        q_ref[:, at] = q
        last_ref[:, at] = q[-NY:]
        passed = layers(jnp.exp(-(absorber * cross_ref[:, at])))
        emitted = layers(p * emission_ref[:, at])
        for k, (tile, depth) in enumerate(zip(to_tiles(*exits(passed, emitted)), depths)):
            rest = tile - tile.astype(jnp.bfloat16).astype(jnp.float32)
            below = jnp.where(depth_lanes(len(passed)), depth, rest)
            exit_ref[k * groups + g] = jnp.concatenate([tile, below], axis=0).astype(jnp.bfloat16)


def scan(exit_of, pass_ref, enter_ref):
    count = enter_ref.shape[0]
    carry = jnp.zeros(enter_ref.shape[1:], jnp.float32)
    upper = top(carry)
    for i in range(count):
        j = count - 1 - i
        enter_ref[i, :HALF] = carry[:HALF]
        enter_ref[j, HALF:] = carry[HALF:]
        carry = jnp.where(upper, pass_ref[i], pass_ref[j]) * carry + jnp.where(
            upper, exit_of(i), exit_of(j)
        )


def first_scan_kernel(axis, count, arrived_ref, cross_ref, enter_ref, pass_ref, exit_ref):
    group = lax.rem(lax.axis_index(axis), cross_ref.shape[0])
    cross = cross_ref[pl.ds(group, 1), :]
    for s in range(arrived_ref.shape[0]):
        arrived = arrived_ref[s].astype(jnp.float32)
        depths = depth_lanes(count)
        exit_ref[s] = arrived[:ROWS] + jnp.where(depths, 0.0, arrived[ROWS:])
        depth = jnp.sum(jnp.where(depths, arrived[ROWS:], 0.0), axis=1, keepdims=True)
        pass_ref[s] = jnp.exp(-(depth * cross))
    scan(lambda at: exit_ref[at], pass_ref, enter_ref)


def response_kernel(axis, count, arrived_ref, cross_ref, emission_ref, same_ref, other_ref):
    group = lax.rem(lax.axis_index(axis), cross_ref.shape[0])
    cross = cross_ref[pl.ds(group, 1), :]
    emission = time_step * emission_ref[pl.ds(group, 1), :]
    lane = lax.broadcasted_iota(jnp.int32, (ROWS, LANES), 1)
    mine = [(lane >= PARTS * k) & (lane < PARTS * (k + 1)) for k in range(count)]
    for s in range(arrived_ref.shape[0]):
        depths = arrived_ref[s].astype(jnp.float32)[ROWS:]
        after = jnp.ones((ROWS, LANES), jnp.float32)
        taken = other = jnp.zeros((ROWS, LANES), jnp.float32)
        for k in reversed(range(count)):
            depth = jnp.sum(jnp.where(mine[k], depths, 0.0), axis=1, keepdims=True)
            t = jnp.exp(-(depth * cross))
            taken = taken + (1.0 - t)
            other = other + (after * after) * (t * (1.0 - t))
            after = after * t
        same_ref[s] = emission * (after * taken)
        other_ref[s] = emission * other


def second_scan_kernel(arrived_ref, entered_ref, pass_ref, same_ref, other_ref, enter_ref, exit_ref):
    for s in range(arrived_ref.shape[0]):
        entered = entered_ref[s]
        exit_ref[s] = (
            arrived_ref[s, ROWS:]
            + same_ref[s] * entered
            + other_ref[s] * pltpu.roll(entered, HALF, 0)
        )
    scan(lambda at: exit_ref[at], pass_ref, enter_ref)


def rate_kernel(axis, pattern_ref, *refs):
    pieces, (table_ref, bracket_ref, out_ref, q_ref) = refs[:-4], refs[-4:]
    brackets, rows, count = table_ref.shape[:3]
    width = pieces[0].shape[1]
    for place, piece in enumerate(pieces):
        q_ref[:, place * width : (place + 1) * width] = piece[...]
    me = lax.axis_index(axis)
    bracket = column(bracket_ref[...])

    def block(r, k):
        source = pattern_ref[k, r]
        place = lax.rem(source, rows) + rows * ((source // rows) ^ me)
        return q_ref[:, pl.ds(pl.multiple_of(place * LANES, LANES), LANES)]

    for r in range(rows):
        picked = jnp.concatenate([block(r, k) for k in range(count)], axis=1)
        both = jnp.concatenate(
            [
                jnp.concatenate([table_ref[b, r, k] for k in range(count)], axis=1)
                for b in range(brackets)
            ],
            axis=0,
        )
        product = lax.dot_general(
            picked, both, (((1,), (1,)), ((), ())), preferred_element_type=jnp.float32
        )
        out_ref[:, r * LANES : (r + 1) * LANES] = jnp.where(
            bracket == 0, product[:, :LANES], product[:, LANES:]
        )


def step_kernel(final, axis, *refs):
    (p_ref, rate_ref, enter_ref, arrived_ref, inflow_ref, cross_ref, emission_ref,
     absorber_ref, stream_ref, crossways_ref) = refs[:10]
    absorber = column(absorber_ref[...])
    along_x = layers(column(stream_ref[...]))
    along_y = column(crossways_ref[...])
    forward_y = layers(jnp.maximum(along_y, 0.0))
    backward_y = layers(jnp.minimum(along_y, 0.0))
    inlet = lax.axis_index(axis) == 0
    groups = p_ref.shape[1] // LANES
    for g in range(groups):
        at = slice(g * LANES, (g + 1) * LANES)
        p = layers(p_ref[:, at])
        emission = emission_ref[:, at]
        emitted = [value * emission for value in p]
        passed = layers(jnp.exp(-(absorber * cross_ref[:, at])))
        entering = get_enters(enter_ref, g, groups) if final else (None, None)
        absorbed = absorbed_of(passed, emitted, *entering)
        boundary = jnp.where(inlet, inflow_ref[:, at], arrived_ref[:, at].astype(jnp.float32))
        carried = advection(p, boundary, along_x, forward_y, backward_y)
        rates = layers(rate_ref[:, at])
        tendency = [q - e + a + v for q, e, a, v in zip(rates, emitted, absorbed, carried)]
        if final:
            start_ref, updated_ref, absorption_ref = refs[10:]
            start = layers(start_ref[:, at])
            for k, rate in enumerate(tendency):
                here = slice(k * NY, (k + 1) * NY)
                updated_ref[here, at] = 0.5 * (start[k] + p[k] + time_step * rate)
                absorption_ref[here, at] = absorbed[k]
        else:
            middle_ref, swap_ref = refs[10:]
            middle = [value + time_step * rate for value, rate in zip(p, tendency)]
            for k, value in enumerate(middle):
                middle_ref[k * NY : (k + 1) * NY, at] = value
            leaving = to_tiles(*exits(passed, [value * emission for value in middle]))
            for k, tile in enumerate(leaving):
                swap_ref[k * groups + g, :ROWS] = enter_ref[k * groups + g]
                swap_ref[k * groups + g, ROWS:] = tile


def middle_kernel(part_ref, swap_ref, cross_ref, absorber_ref, middle_ref, q_ref, last_ref):
    absorber = column(absorber_ref[...])
    groups = part_ref.shape[1] // LANES
    for g in range(groups):
        at = slice(g * LANES, (g + 1) * LANES)
        part = layers(part_ref[:, at])
        passed = layers(jnp.exp(-(absorber * cross_ref[:, at])))
        downward, upward = get_enters(swap_ref, g, groups)
        count = len(passed)
        down, up = [None] * count, [None] * count
        for k in range(count):
            downward = passed[k] * downward
            down[k] = downward
        for k in reversed(range(count)):
            upward = passed[k] * upward
            up[k] = upward
        for k in range(count):
            here = slice(k * NY, (k + 1) * NY)
            value = part[k] + time_step * ((1.0 - passed[k]) * (down[k] + up[k]))
            middle_ref[here, at] = value
            q_ref[here, at] = value.astype(jnp.bfloat16)
            if k == count - 1:
                last_ref[:, at] = value.astype(jnp.bfloat16)


def vmem(count):
    return [pl.BlockSpec(memory_space=pltpu.VMEM)] * count


LIMIT = pltpu.CompilerParams(vmem_limit_bytes=24 * 2**20)


def call(body, args, outs, cost, scratch=(), in_specs=None, params=LIMIT):
    return pl.pallas_call(
        body,
        out_shape=outs,
        in_specs=in_specs or vmem(len(args)),
        out_specs=vmem(len(outs)),
        scratch_shapes=scratch,
        compiler_params=params,
        cost_estimate=pl.CostEstimate(flops=cost, bytes_accessed=cost, transcendentals=0),
    )(*args)


def gathered(q, axis):
    def swap(value, apart):
        return lax.ppermute(value, axis, [(i, i ^ apart) for i in range(lax.axis_size(axis))])

    far = swap(q, 2)
    return q, swap(q, 1), far, swap(far, 1)


def rate_term(pieces, rate_blocks, pattern, bracket):
    cells, levels = pieces[0].shape
    return pl.pallas_call(
        functools.partial(rate_kernel, "lev"),
        in_specs=[pl.BlockSpec(memory_space=pltpu.SMEM)] + vmem(len(pieces) + 2),
        out_specs=pl.BlockSpec(memory_space=pltpu.VMEM),
        out_shape=jax.ShapeDtypeStruct((cells, levels), jnp.float32),
        scratch_shapes=[pltpu.VMEM((cells, len(pieces) * levels), jnp.bfloat16)],
        compiler_params=LIMIT,
        cost_estimate=pl.CostEstimate(
            flops=2 * cells * rate_blocks.size, bytes_accessed=2 * rate_blocks.size, transcendentals=0
        ),
    )(pattern, *pieces, rate_blocks, bracket)


def shifted(value, axis):
    peers = lax.axis_size(axis)
    return lax.ppermute(value, axis, [(i, i + 1) for i in range(peers - 1)])


def local(
    populations,
    rate_blocks,
    pattern,
    bracket,
    cross_section,
    emission,
    absorber,
    stream_speed,
    cross_speed,
    inflow,
):
    cells, levels = populations.shape
    strips = lax.axis_size("cell")
    bracket = bracket.reshape(1, cells)
    pattern = pattern.T
    cross = cross_section.reshape(1, levels)
    crosses = cross_section.reshape(levels // LANES, LANES)
    emission = emission.reshape(1, levels)
    absorber = absorber.reshape(1, cells)
    stream = stream_speed.reshape(1, cells)
    crossways = cross_speed.reshape(1, cells)

    field = jax.ShapeDtypeStruct((cells, levels), jnp.float32)
    rounded = jax.ShapeDtypeStruct((cells, levels), jnp.bfloat16)
    layer = jax.ShapeDtypeStruct((NY, levels), jnp.bfloat16)
    tiles = jax.ShapeDtypeStruct((strips, ROWS, LANES), jnp.float32)
    size = cells * levels * 4

    def swap(value):
        return lax.all_to_all(value, "cell", 0, 0, tiled=True)

    sources = (populations, cross, emission, absorber)
    q, last, leaving = call(
        first_kernel,
        sources,
        (rounded, layer, jax.ShapeDtypeStruct((strips, 2 * ROWS, LANES), jnp.bfloat16)),
        LONG * size,
        [pltpu.VMEM(value.shape, value.dtype) for value in sources]
        + [pltpu.SemaphoreType.DMA((len(sources),))],
        [pl.BlockSpec(memory_space=pl.ANY)] * len(sources),
        pltpu.CompilerParams(vmem_limit_bytes=FIRST * 2**20),
    )
    pieces = gathered(q, "lev")
    arrived = shifted(last, "cell")
    sent, rates = lax.optimization_barrier(
        (swap(leaving), rate_term(pieces, rate_blocks, pattern, bracket))
    )
    entered, passes = call(
        functools.partial(first_scan_kernel, "cell", cells // NY),
        (sent, crosses),
        (tiles, tiles),
        size,
        [pltpu.VMEM(tiles.shape, jnp.float32)],
    )
    same, other = call(
        functools.partial(response_kernel, "cell", cells // NY),
        (sent, crosses, emission.reshape(crosses.shape)),
        (tiles, tiles),
        size,
    )
    part, leaving = call(
        functools.partial(step_kernel, False, "cell"),
        (populations, rates, entered, arrived, inflow, cross, emission, absorber, stream, crossways),
        (field, jax.ShapeDtypeStruct((strips, 2 * ROWS, LANES), jnp.float32)),
        5 * size,
    )
    swapped = swap(leaving)
    middle, q, last = call(
        middle_kernel, (part, swapped, cross, absorber), (field, rounded, layer), 3 * size
    )
    pieces = gathered(q, "lev")
    arrived = shifted(last, "cell")
    (entering,) = call(
        second_scan_kernel,
        (swapped, entered, passes, same, other),
        (tiles,),
        size,
        [pltpu.VMEM(tiles.shape, jnp.float32)],
    )
    entering = swap(entering)
    rates = rate_term(pieces, rate_blocks, pattern, bracket)
    return call(
        functools.partial(step_kernel, True, "cell"),
        (middle, rates, entering, arrived, inflow, cross, emission, absorber, stream, crossways, populations),
        (field, field),
        5 * size,
    )


def solution(mesh):
    in_specs = (
        P("cell", "lev"),
        P(None, "lev", None, None, None),
        P("lev", None),
        P("cell"),
        P("lev"),
        P("lev"),
        P("cell"),
        P("cell"),
        P("cell"),
        P(None, "lev"),
    )
    out_specs = (P("cell", "lev"), P("cell", "lev"))
    return jax.shard_map(local, mesh=mesh, in_specs=in_specs, out_specs=out_specs, check_vma=False)
```

```python
import functools

import jax
import jax.numpy as jnp
from jax import lax
from jax.experimental import pallas as pl
from jax.experimental.pallas import tpu as pltpu
from jax.sharding import PartitionSpec as P

NY = 16
LANES = 128
ROWS = 8
HALF = 4
PARTS = 2
FIRST = 57
LONG = 40000
time_step = 0.25


def column(row):
    n = row.shape[1]
    at_row = lax.broadcasted_iota(jnp.int32, (n, n), 0)
    at_column = lax.broadcasted_iota(jnp.int32, (n, n), 1)
    return jnp.sum(jnp.where(at_row == at_column, row, jnp.zeros_like(row)), axis=1, keepdims=True)


def layers(value):
    return [value[k : k + NY] for k in range(0, value.shape[0], NY)]


def exits(passed, emitted):
    down, up = emitted[0], emitted[-1]
    for t, e in zip(passed[1:], emitted[1:]):
        down = t * down + e
    for t, e in zip(passed[-2::-1], emitted[-2::-1]):
        up = t * up + e
    return down, up


def top(value):
    return lax.broadcasted_iota(jnp.int32, value.shape, 0) < HALF


def to_tiles(down, up):
    tiles = []
    for k in range(0, NY, ROWS):
        d, u = down[k : k + ROWS], up[k : k + ROWS]
        tiles.append(jnp.where(top(d), d, pltpu.roll(u, HALF, 0)))
        tiles.append(jnp.where(top(d), pltpu.roll(d, HALF, 0), u))
    return tiles


def from_tiles(tiles):
    down, up = [], []
    for first, second in zip(tiles[::2], tiles[1::2]):
        down.append(jnp.where(top(first), first, pltpu.roll(second, HALF, 0)))
        up.append(jnp.where(top(first), pltpu.roll(first, HALF, 0), second))
    return jnp.concatenate(down, axis=0), jnp.concatenate(up, axis=0)


def get_enters(enter_ref, group, groups):
    return from_tiles([enter_ref[k * groups + group, :ROWS] for k in range(NY // HALF)])


def depth_tiles(absorber):
    lane = lax.broadcasted_iota(jnp.int32, (NY, LANES), 1)
    by_layer = layers(absorber)
    count = len(by_layer)
    forward = reverse = jnp.zeros((NY, LANES), jnp.float32)
    for k, value in enumerate(by_layer):
        high = value.astype(jnp.bfloat16).astype(jnp.float32)
        for j, part in enumerate((high, value - high)):
            forward = jnp.where(lane == PARTS * k + j, part, forward)
            reverse = jnp.where(lane == PARTS * (count - 1 - k) + j, part, reverse)
    return to_tiles(forward, reverse)


def absorbed_of(passed, emitted, enter_down, enter_up):
    count = len(passed)
    downward, upward = [None] * count, [None] * count
    running = enter_down
    for k in range(count):
        running = emitted[k] if running is None else passed[k] * running + emitted[k]
        downward[k] = running
    running = enter_up
    for k in reversed(range(count)):
        running = emitted[k] if running is None else passed[k] * running + emitted[k]
        upward[k] = running
    return [
        (1.0 - t) * (d + u - 2.0 * e) for t, d, u, e in zip(passed, downward, upward, emitted)
    ]


def advection(layered, boundary, along_x, forward_y, backward_y):
    result, upstream = [], boundary
    for k, here in enumerate(layered):
        before = pltpu.roll(here, 1, 0)
        after = pltpu.roll(here, NY - 1, 0)
        result.append(
            -along_x[k] * (here - upstream) - forward_y[k] * (here - before) - backward_y[k] * (after - here)
        )
        upstream = here
    return result


def depth_lanes(count):
    return lax.broadcasted_iota(jnp.int32, (ROWS, LANES), 1) < PARTS * count


def first_kernel(p_hbm, cross_hbm, emission_hbm, absorber_hbm, q_ref, last_ref, exit_ref, *scratch):
    sems = scratch[-1]
    copies = [
        pltpu.make_async_copy(source, target, sems.at[i])
        for i, (source, target) in enumerate(
            zip((p_hbm, cross_hbm, emission_hbm, absorber_hbm), scratch[:-1])
        )
    ]
    for copy in copies:
        copy.start()
    for copy in copies:
        copy.wait()
    p_ref, cross_ref, emission_ref, absorber_ref = scratch[:-1]
    absorber = column(absorber_ref[...])
    depths = depth_tiles(absorber)
    groups = p_ref.shape[1] // LANES
    for g in range(groups):
        at = slice(g * LANES, (g + 1) * LANES)
        p = p_ref[:, at]
        q = p.astype(jnp.bfloat16)
        q_ref[:, at] = q
        last_ref[:, at] = q[-NY:]
        passed = layers(jnp.exp(-(absorber * cross_ref[:, at])))
        emitted = layers(p * emission_ref[:, at])
        for k, (tile, depth) in enumerate(zip(to_tiles(*exits(passed, emitted)), depths)):
            rest = tile - tile.astype(jnp.bfloat16).astype(jnp.float32)
            below = jnp.where(depth_lanes(len(passed)), depth, rest)
            exit_ref[k * groups + g] = jnp.concatenate([tile, below], axis=0).astype(jnp.bfloat16)


def scan(exit_of, pass_ref, enter_ref):
    count = enter_ref.shape[0]
    carry = jnp.zeros(enter_ref.shape[1:], jnp.float32)
    upper = top(carry)
    for i in range(count):
        j = count - 1 - i
        enter_ref[i, :HALF] = carry[:HALF]
        enter_ref[j, HALF:] = carry[HALF:]
        carry = jnp.where(upper, pass_ref[i], pass_ref[j]) * carry + jnp.where(
            upper, exit_of(i), exit_of(j)
        )


def first_scan_kernel(axis, count, arrived_ref, cross_ref, enter_ref, pass_ref, exit_ref):
    group = lax.rem(lax.axis_index(axis), cross_ref.shape[0])
    cross = cross_ref[pl.ds(group, 1), :]
    for s in range(arrived_ref.shape[0]):
        arrived = arrived_ref[s].astype(jnp.float32)
        depths = depth_lanes(count)
        exit_ref[s] = arrived[:ROWS] + jnp.where(depths, 0.0, arrived[ROWS:])
        depth = jnp.sum(jnp.where(depths, arrived[ROWS:], 0.0), axis=1, keepdims=True)
        pass_ref[s] = jnp.exp(-(depth * cross))
    scan(lambda at: exit_ref[at], pass_ref, enter_ref)


def response_kernel(axis, count, arrived_ref, cross_ref, emission_ref, same_ref, other_ref):
    group = lax.rem(lax.axis_index(axis), cross_ref.shape[0])
    cross = cross_ref[pl.ds(group, 1), :]
    emission = time_step * emission_ref[pl.ds(group, 1), :]
    lane = lax.broadcasted_iota(jnp.int32, (ROWS, LANES), 1)
    mine = [(lane >= PARTS * k) & (lane < PARTS * (k + 1)) for k in range(count)]
    for s in range(arrived_ref.shape[0]):
        depths = arrived_ref[s].astype(jnp.float32)[ROWS:]
        after = jnp.ones((ROWS, LANES), jnp.float32)
        taken = other = jnp.zeros((ROWS, LANES), jnp.float32)
        for k in reversed(range(count)):
            depth = jnp.sum(jnp.where(mine[k], depths, 0.0), axis=1, keepdims=True)
            t = jnp.exp(-(depth * cross))
            taken = taken + (1.0 - t)
            other = other + (after * after) * (t * (1.0 - t))
            after = after * t
        same_ref[s] = emission * (after * taken)
        other_ref[s] = emission * other


def second_scan_kernel(arrived_ref, entered_ref, pass_ref, same_ref, other_ref, enter_ref, exit_ref):
    for s in range(arrived_ref.shape[0]):
        entered = entered_ref[s]
        exit_ref[s] = (
            arrived_ref[s, ROWS:]
            + same_ref[s] * entered
            + other_ref[s] * pltpu.roll(entered, HALF, 0)
        )
    scan(lambda at: exit_ref[at], pass_ref, enter_ref)


def first_bracket_kernel(bracket_ref, first_ref):
    first = jnp.where(column(bracket_ref[...]) == 0, 1.0, 0.0)
    first_ref[...] = jnp.broadcast_to(first, first_ref.shape)


def rate_kernel(axis, pattern_ref, *refs):
    pieces, (table_ref, first_ref, out_ref, q_ref) = refs[:-4], refs[-4:]
    brackets, rows, count = table_ref.shape[:3]
    width = pieces[0].shape[1]
    for place, piece in enumerate(pieces):
        q_ref[:, place * width : (place + 1) * width] = piece[...]
    me = lax.axis_index(axis)
    first = first_ref[...] > 0.5

    def block(r, k):
        source = pattern_ref[k, r]
        place = lax.rem(source, rows) + rows * ((source // rows) ^ me)
        return q_ref[:, pl.ds(pl.multiple_of(place * LANES, LANES), LANES)]

    for r in range(rows):
        picked = jnp.concatenate([block(r, k) for k in range(count)], axis=1)
        both = jnp.concatenate(
            [
                jnp.concatenate([table_ref[b, r, k] for k in range(count)], axis=1)
                for b in range(brackets)
            ],
            axis=0,
        )
        product = lax.dot_general(
            picked, both, (((1,), (1,)), ((), ())), preferred_element_type=jnp.float32
        )
        out_ref[:, r * LANES : (r + 1) * LANES] = jnp.where(
            first, product[:, :LANES], product[:, LANES:]
        )


def step_kernel(final, axis, *refs):
    (p_ref, rate_ref, enter_ref, arrived_ref, inflow_ref, cross_ref, emission_ref,
     absorber_ref, stream_ref, crossways_ref) = refs[:10]
    absorber = column(absorber_ref[...])
    along_x = layers(column(stream_ref[...]))
    along_y = column(crossways_ref[...])
    forward_y = layers(jnp.maximum(along_y, 0.0))
    backward_y = layers(jnp.minimum(along_y, 0.0))
    inlet = lax.axis_index(axis) == 0
    groups = p_ref.shape[1] // LANES
    for g in range(groups):
        at = slice(g * LANES, (g + 1) * LANES)
        p = layers(p_ref[:, at])
        emission = emission_ref[:, at]
        emitted = [value * emission for value in p]
        passed = layers(jnp.exp(-(absorber * cross_ref[:, at])))
        entering = get_enters(enter_ref, g, groups) if final else (None, None)
        absorbed = absorbed_of(passed, emitted, *entering)
        boundary = jnp.where(inlet, inflow_ref[:, at], arrived_ref[:, at].astype(jnp.float32))
        carried = advection(p, boundary, along_x, forward_y, backward_y)
        rates = layers(rate_ref[:, at])
        tendency = [q - e + a + v for q, e, a, v in zip(rates, emitted, absorbed, carried)]
        if final:
            start_ref, updated_ref, absorption_ref = refs[10:]
            start = layers(start_ref[:, at])
            for k, rate in enumerate(tendency):
                here = slice(k * NY, (k + 1) * NY)
                updated_ref[here, at] = 0.5 * (start[k] + p[k] + time_step * rate)
                absorption_ref[here, at] = absorbed[k]
        else:
            middle_ref, swap_ref = refs[10:]
            middle = [value + time_step * rate for value, rate in zip(p, tendency)]
            for k, value in enumerate(middle):
                middle_ref[k * NY : (k + 1) * NY, at] = value
            leaving = to_tiles(*exits(passed, [value * emission for value in middle]))
            for k, tile in enumerate(leaving):
                swap_ref[k * groups + g, :ROWS] = enter_ref[k * groups + g]
                swap_ref[k * groups + g, ROWS:] = tile


def middle_kernel(part_ref, swap_ref, cross_ref, absorber_ref, middle_ref, q_ref, last_ref):
    absorber = column(absorber_ref[...])
    groups = part_ref.shape[1] // LANES
    for g in range(groups):
        at = slice(g * LANES, (g + 1) * LANES)
        part = layers(part_ref[:, at])
        passed = layers(jnp.exp(-(absorber * cross_ref[:, at])))
        downward, upward = get_enters(swap_ref, g, groups)
        count = len(passed)
        down, up = [None] * count, [None] * count
        for k in range(count):
            downward = passed[k] * downward
            down[k] = downward
        for k in reversed(range(count)):
            upward = passed[k] * upward
            up[k] = upward
        for k in range(count):
            here = slice(k * NY, (k + 1) * NY)
            value = part[k] + time_step * ((1.0 - passed[k]) * (down[k] + up[k]))
            middle_ref[here, at] = value
            q_ref[here, at] = value.astype(jnp.bfloat16)
            if k == count - 1:
                last_ref[:, at] = value.astype(jnp.bfloat16)


def vmem(count):
    return [pl.BlockSpec(memory_space=pltpu.VMEM)] * count


LIMIT = pltpu.CompilerParams(vmem_limit_bytes=24 * 2**20)


def call(body, args, outs, cost, scratch=(), in_specs=None, params=LIMIT):
    return pl.pallas_call(
        body,
        out_shape=outs,
        in_specs=in_specs or vmem(len(args)),
        out_specs=vmem(len(outs)),
        scratch_shapes=scratch,
        compiler_params=params,
        cost_estimate=pl.CostEstimate(flops=cost, bytes_accessed=cost, transcendentals=0),
    )(*args)


def gathered(q, axis):
    def swap(value, apart):
        return lax.ppermute(value, axis, [(i, i ^ apart) for i in range(lax.axis_size(axis))])

    far = swap(q, 2)
    return q, swap(q, 1), far, swap(far, 1)


def rate_term(pieces, rate_blocks, pattern, first):
    cells, levels = pieces[0].shape
    return pl.pallas_call(
        functools.partial(rate_kernel, "lev"),
        in_specs=[pl.BlockSpec(memory_space=pltpu.SMEM)] + vmem(len(pieces) + 2),
        out_specs=pl.BlockSpec(memory_space=pltpu.VMEM),
        out_shape=jax.ShapeDtypeStruct((cells, levels), jnp.float32),
        scratch_shapes=[pltpu.VMEM((cells, len(pieces) * levels), jnp.bfloat16)],
        compiler_params=LIMIT,
        cost_estimate=pl.CostEstimate(
            flops=2 * cells * rate_blocks.size, bytes_accessed=2 * rate_blocks.size, transcendentals=0
        ),
    )(pattern, *pieces, rate_blocks, first)


def shifted(value, axis):
    peers = lax.axis_size(axis)
    return lax.ppermute(value, axis, [(i, i + 1) for i in range(peers - 1)])


def local(
    populations,
    rate_blocks,
    pattern,
    bracket,
    cross_section,
    emission,
    absorber,
    stream_speed,
    cross_speed,
    inflow,
):
    cells, levels = populations.shape
    strips = lax.axis_size("cell")
    bracket = bracket.reshape(1, cells)
    pattern = pattern.T
    cross = cross_section.reshape(1, levels)
    crosses = cross_section.reshape(levels // LANES, LANES)
    emission = emission.reshape(1, levels)
    absorber = absorber.reshape(1, cells)
    stream = stream_speed.reshape(1, cells)
    crossways = cross_speed.reshape(1, cells)

    field = jax.ShapeDtypeStruct((cells, levels), jnp.float32)
    rounded = jax.ShapeDtypeStruct((cells, levels), jnp.bfloat16)
    layer = jax.ShapeDtypeStruct((NY, levels), jnp.bfloat16)
    tiles = jax.ShapeDtypeStruct((strips, ROWS, LANES), jnp.float32)
    size = cells * levels * 4

    def swap(value):
        return lax.all_to_all(value, "cell", 0, 0, tiled=True)

    sources = (populations, cross, emission, absorber)
    q, last, leaving = call(
        first_kernel,
        sources,
        (rounded, layer, jax.ShapeDtypeStruct((strips, 2 * ROWS, LANES), jnp.bfloat16)),
        LONG * size,
        [pltpu.VMEM(value.shape, value.dtype) for value in sources]
        + [pltpu.SemaphoreType.DMA((len(sources),))],
        [pl.BlockSpec(memory_space=pl.ANY)] * len(sources),
        pltpu.CompilerParams(vmem_limit_bytes=FIRST * 2**20),
    )
    pieces = gathered(q, "lev")
    (first,) = call(
        first_bracket_kernel,
        (bracket,),
        (jax.ShapeDtypeStruct((cells, LANES), jnp.float32),),
        LONG * size,
    )
    last, first = lax.optimization_barrier((last, first))
    arrived = shifted(last, "cell")
    sent, rates = lax.optimization_barrier(
        (swap(leaving), rate_term(pieces, rate_blocks, pattern, first))
    )
    entered, passes = call(
        functools.partial(first_scan_kernel, "cell", cells // NY),
        (sent, crosses),
        (tiles, tiles),
        size,
        [pltpu.VMEM(tiles.shape, jnp.float32)],
    )
    same, other = call(
        functools.partial(response_kernel, "cell", cells // NY),
        (sent, crosses, emission.reshape(crosses.shape)),
        (tiles, tiles),
        size,
    )
    part, leaving = call(
        functools.partial(step_kernel, False, "cell"),
        (populations, rates, entered, arrived, inflow, cross, emission, absorber, stream, crossways),
        (field, jax.ShapeDtypeStruct((strips, 2 * ROWS, LANES), jnp.float32)),
        5 * size,
    )
    swapped = swap(leaving)
    middle, q, last = call(
        middle_kernel, (part, swapped, cross, absorber), (field, rounded, layer), 3 * size
    )
    pieces = gathered(q, "lev")
    arrived = shifted(last, "cell")
    (entering,) = call(
        second_scan_kernel,
        (swapped, entered, passes, same, other),
        (tiles,),
        size,
        [pltpu.VMEM(tiles.shape, jnp.float32)],
    )
    entering = swap(entering)
    rates = rate_term(pieces, rate_blocks, pattern, first)
    return call(
        functools.partial(step_kernel, True, "cell"),
        (middle, rates, entering, arrived, inflow, cross, emission, absorber, stream, crossways, populations),
        (field, field),
        5 * size,
    )


def solution(mesh):
    in_specs = (
        P("cell", "lev"),
        P(None, "lev", None, None, None),
        P("lev", None),
        P("cell"),
        P("lev"),
        P("lev"),
        P("cell"),
        P("cell"),
        P("cell"),
        P(None, "lev"),
    )
    out_specs = (P("cell", "lev"), P("cell", "lev"))
    return jax.shard_map(local, mesh=mesh, in_specs=in_specs, out_specs=out_specs, check_vma=False)
```

```python
import functools

import jax
import jax.numpy as jnp
from jax import lax
from jax.experimental import pallas as pl
from jax.experimental.pallas import tpu as pltpu
from jax.sharding import PartitionSpec as P

NY = 16
LANES = 128
ROWS = 8
HALF = 4
PARTS = 2
FIRST = 57
LONG = 40000
CHUNKS = 4
time_step = 0.25


def column(row):
    n = row.shape[1]
    at_row = lax.broadcasted_iota(jnp.int32, (n, n), 0)
    at_column = lax.broadcasted_iota(jnp.int32, (n, n), 1)
    return jnp.sum(jnp.where(at_row == at_column, row, jnp.zeros_like(row)), axis=1, keepdims=True)


def layers(value):
    return [value[k : k + NY] for k in range(0, value.shape[0], NY)]


def exits(passed, emitted):
    down, up = emitted[0], emitted[-1]
    for t, e in zip(passed[1:], emitted[1:]):
        down = t * down + e
    for t, e in zip(passed[-2::-1], emitted[-2::-1]):
        up = t * up + e
    return down, up


def top(value):
    return lax.broadcasted_iota(jnp.int32, value.shape, 0) < HALF


def to_tiles(down, up):
    tiles = []
    for k in range(0, NY, ROWS):
        d, u = down[k : k + ROWS], up[k : k + ROWS]
        tiles.append(jnp.where(top(d), d, pltpu.roll(u, HALF, 0)))
        tiles.append(jnp.where(top(d), pltpu.roll(d, HALF, 0), u))
    return tiles


def from_tiles(tiles):
    down, up = [], []
    for first, second in zip(tiles[::2], tiles[1::2]):
        down.append(jnp.where(top(first), first, pltpu.roll(second, HALF, 0)))
        up.append(jnp.where(top(first), pltpu.roll(first, HALF, 0), second))
    return jnp.concatenate(down, axis=0), jnp.concatenate(up, axis=0)


def get_enters(enter_ref, group, groups):
    return from_tiles([enter_ref[k * groups + group, :ROWS] for k in range(NY // HALF)])


def depth_tiles(absorber):
    lane = lax.broadcasted_iota(jnp.int32, (NY, LANES), 1)
    by_layer = layers(absorber)
    count = len(by_layer)
    forward = reverse = jnp.zeros((NY, LANES), jnp.float32)
    for k, value in enumerate(by_layer):
        high = value.astype(jnp.bfloat16).astype(jnp.float32)
        for j, part in enumerate((high, value - high)):
            forward = jnp.where(lane == PARTS * k + j, part, forward)
            reverse = jnp.where(lane == PARTS * (count - 1 - k) + j, part, reverse)
    return to_tiles(forward, reverse)


def absorbed_of(passed, emitted, enter_down, enter_up):
    count = len(passed)
    downward, upward = [None] * count, [None] * count
    running = enter_down
    for k in range(count):
        running = emitted[k] if running is None else passed[k] * running + emitted[k]
        downward[k] = running
    running = enter_up
    for k in reversed(range(count)):
        running = emitted[k] if running is None else passed[k] * running + emitted[k]
        upward[k] = running
    return [
        (1.0 - t) * (d + u - 2.0 * e) for t, d, u, e in zip(passed, downward, upward, emitted)
    ]


def advection(layered, boundary, along_x, forward_y, backward_y):
    result, upstream = [], boundary
    for k, here in enumerate(layered):
        before = pltpu.roll(here, 1, 0)
        after = pltpu.roll(here, NY - 1, 0)
        result.append(
            -along_x[k] * (here - upstream) - forward_y[k] * (here - before) - backward_y[k] * (after - here)
        )
        upstream = here
    return result


def depth_lanes(count):
    return lax.broadcasted_iota(jnp.int32, (ROWS, LANES), 1) < PARTS * count


def first_kernel(p_hbm, cross_hbm, emission_hbm, absorber_hbm, q_ref, last_ref, exit_ref, *scratch):
    sems = scratch[-1]
    p_ref, cross_ref, emission_ref, absorber_ref = scratch[:-1]
    small = [
        pltpu.make_async_copy(source, target, sems.at[CHUNKS + i])
        for i, (source, target) in enumerate(
            ((absorber_hbm, absorber_ref), (cross_hbm, cross_ref), (emission_hbm, emission_ref))
        )
    ]
    width = p_ref.shape[1] // CHUNKS
    large = [
        pltpu.make_async_copy(
            p_hbm.at[:, c * width : (c + 1) * width], p_ref.at[:, c * width : (c + 1) * width], sems.at[c]
        )
        for c in range(CHUNKS)
    ]
    for copy in (*small, *large):
        copy.start()
    for copy in small:
        copy.wait()
    absorber = column(absorber_ref[...])
    depths = depth_tiles(absorber)
    groups = p_ref.shape[1] // LANES
    for g in range(groups):
        at = slice(g * LANES, (g + 1) * LANES)
        if g * LANES % width == 0:
            large[g * LANES // width].wait()
        p = p_ref[:, at]
        q = p.astype(jnp.bfloat16)
        q_ref[:, at] = q
        last_ref[:, at] = q[-NY:]
        passed = layers(jnp.exp(-(absorber * cross_ref[:, at])))
        emitted = layers(p * emission_ref[:, at])
        for k, (tile, depth) in enumerate(zip(to_tiles(*exits(passed, emitted)), depths)):
            rest = tile - tile.astype(jnp.bfloat16).astype(jnp.float32)
            below = jnp.where(depth_lanes(len(passed)), depth, rest)
            exit_ref[k * groups + g] = jnp.concatenate([tile, below], axis=0).astype(jnp.bfloat16)


def scan(exit_of, pass_ref, enter_ref):
    count = enter_ref.shape[0]
    carry = jnp.zeros(enter_ref.shape[1:], jnp.float32)
    upper = top(carry)
    for i in range(count):
        j = count - 1 - i
        enter_ref[i, :HALF] = carry[:HALF]
        enter_ref[j, HALF:] = carry[HALF:]
        carry = jnp.where(upper, pass_ref[i], pass_ref[j]) * carry + jnp.where(
            upper, exit_of(i), exit_of(j)
        )


def first_scan_kernel(axis, count, arrived_ref, cross_ref, enter_ref, pass_ref, exit_ref):
    group = lax.rem(lax.axis_index(axis), cross_ref.shape[0])
    cross = cross_ref[pl.ds(group, 1), :]
    for s in range(arrived_ref.shape[0]):
        arrived = arrived_ref[s].astype(jnp.float32)
        depths = depth_lanes(count)
        exit_ref[s] = arrived[:ROWS] + jnp.where(depths, 0.0, arrived[ROWS:])
        depth = jnp.sum(jnp.where(depths, arrived[ROWS:], 0.0), axis=1, keepdims=True)
        pass_ref[s] = jnp.exp(-(depth * cross))
    scan(lambda at: exit_ref[at], pass_ref, enter_ref)


def response_kernel(axis, count, arrived_ref, cross_ref, emission_ref, same_ref, other_ref):
    group = lax.rem(lax.axis_index(axis), cross_ref.shape[0])
    cross = cross_ref[pl.ds(group, 1), :]
    emission = time_step * emission_ref[pl.ds(group, 1), :]
    lane = lax.broadcasted_iota(jnp.int32, (ROWS, LANES), 1)
    mine = [(lane >= PARTS * k) & (lane < PARTS * (k + 1)) for k in range(count)]
    for s in range(arrived_ref.shape[0]):
        depths = arrived_ref[s].astype(jnp.float32)[ROWS:]
        after = jnp.ones((ROWS, LANES), jnp.float32)
        taken = other = jnp.zeros((ROWS, LANES), jnp.float32)
        for k in reversed(range(count)):
            depth = jnp.sum(jnp.where(mine[k], depths, 0.0), axis=1, keepdims=True)
            t = jnp.exp(-(depth * cross))
            taken = taken + (1.0 - t)
            other = other + (after * after) * (t * (1.0 - t))
            after = after * t
        same_ref[s] = emission * (after * taken)
        other_ref[s] = emission * other


def second_scan_kernel(arrived_ref, entered_ref, pass_ref, same_ref, other_ref, enter_ref, exit_ref):
    for s in range(arrived_ref.shape[0]):
        entered = entered_ref[s]
        exit_ref[s] = (
            arrived_ref[s, ROWS:]
            + same_ref[s] * entered
            + other_ref[s] * pltpu.roll(entered, HALF, 0)
        )
    scan(lambda at: exit_ref[at], pass_ref, enter_ref)


def first_bracket_kernel(bracket_ref, first_ref):
    first = jnp.where(column(bracket_ref[...]) == 0, 1.0, 0.0)
    first_ref[...] = jnp.broadcast_to(first, first_ref.shape)


def rate_kernel(axis, pattern_ref, *refs):
    pieces, (table_ref, first_ref, out_ref, q_ref) = refs[:-4], refs[-4:]
    brackets, rows, count = table_ref.shape[:3]
    width = pieces[0].shape[1]
    for place, piece in enumerate(pieces):
        q_ref[:, place * width : (place + 1) * width] = piece[...]
    me = lax.axis_index(axis)
    first = first_ref[...] > 0.5

    def block(r, k):
        source = pattern_ref[k, r]
        place = lax.rem(source, rows) + rows * ((source // rows) ^ me)
        return q_ref[:, pl.ds(pl.multiple_of(place * LANES, LANES), LANES)]

    for r in range(rows):
        picked = jnp.concatenate([block(r, k) for k in range(count)], axis=1)
        both = jnp.concatenate(
            [
                jnp.concatenate([table_ref[b, r, k] for k in range(count)], axis=1)
                for b in range(brackets)
            ],
            axis=0,
        )
        product = lax.dot_general(
            picked, both, (((1,), (1,)), ((), ())), preferred_element_type=jnp.float32
        )
        out_ref[:, r * LANES : (r + 1) * LANES] = jnp.where(
            first, product[:, :LANES], product[:, LANES:]
        )


def step_kernel(final, axis, *refs):
    (p_ref, rate_ref, enter_ref, arrived_ref, inflow_ref, cross_ref, emission_ref,
     absorber_ref, stream_ref, crossways_ref) = refs[:10]
    absorber = column(absorber_ref[...])
    along_x = layers(column(stream_ref[...]))
    along_y = column(crossways_ref[...])
    forward_y = layers(jnp.maximum(along_y, 0.0))
    backward_y = layers(jnp.minimum(along_y, 0.0))
    inlet = lax.axis_index(axis) == 0
    groups = p_ref.shape[1] // LANES
    copies = []
    for g in range(groups):
        at = slice(g * LANES, (g + 1) * LANES)
        p = layers(p_ref[:, at])
        emission = emission_ref[:, at]
        emitted = [value * emission for value in p]
        passed = layers(jnp.exp(-(absorber * cross_ref[:, at])))
        entering = get_enters(enter_ref, g, groups) if final else (None, None)
        absorbed = absorbed_of(passed, emitted, *entering)
        boundary = jnp.where(inlet, inflow_ref[:, at], arrived_ref[:, at].astype(jnp.float32))
        carried = advection(p, boundary, along_x, forward_y, backward_y)
        rates = layers(rate_ref[:, at])
        tendency = [q - e + a + v for q, e, a, v in zip(rates, emitted, absorbed, carried)]
        if final:
            start_ref, updated_hbm, absorption_hbm, updated_ref, absorption_ref, sems = refs[10:]
            start = layers(start_ref[:, at])
            for k, rate in enumerate(tendency):
                here = slice(k * NY, (k + 1) * NY)
                updated_ref[here, at] = 0.5 * (start[k] + p[k] + time_step * rate)
                absorption_ref[here, at] = absorbed[k]
            width = p_ref.shape[1] // CHUNKS
            if (g + 1) * LANES % width == 0:
                c = (g + 1) * LANES // width - 1
                part = slice(c * width, (c + 1) * width)
                for i, (source, target) in enumerate(
                    ((updated_ref, updated_hbm), (absorption_ref, absorption_hbm))
                ):
                    copy = pltpu.make_async_copy(source.at[:, part], target.at[:, part], sems.at[i, c])
                    copy.start()
                    copies.append(copy)
        else:
            middle_ref, swap_ref = refs[10:]
            middle = [value + time_step * rate for value, rate in zip(p, tendency)]
            for k, value in enumerate(middle):
                middle_ref[k * NY : (k + 1) * NY, at] = value
            leaving = to_tiles(*exits(passed, [value * emission for value in middle]))
            for k, tile in enumerate(leaving):
                swap_ref[k * groups + g, :ROWS] = enter_ref[k * groups + g]
                swap_ref[k * groups + g, ROWS:] = tile
    for copy in copies:
        copy.wait()


def middle_kernel(part_ref, swap_ref, cross_ref, absorber_ref, middle_ref, q_ref, last_ref):
    absorber = column(absorber_ref[...])
    groups = part_ref.shape[1] // LANES
    for g in range(groups):
        at = slice(g * LANES, (g + 1) * LANES)
        part = layers(part_ref[:, at])
        passed = layers(jnp.exp(-(absorber * cross_ref[:, at])))
        downward, upward = get_enters(swap_ref, g, groups)
        count = len(passed)
        down, up = [None] * count, [None] * count
        for k in range(count):
            downward = passed[k] * downward
            down[k] = downward
        for k in reversed(range(count)):
            upward = passed[k] * upward
            up[k] = upward
        for k in range(count):
            here = slice(k * NY, (k + 1) * NY)
            value = part[k] + time_step * ((1.0 - passed[k]) * (down[k] + up[k]))
            middle_ref[here, at] = value
            q_ref[here, at] = value.astype(jnp.bfloat16)
            if k == count - 1:
                last_ref[:, at] = value.astype(jnp.bfloat16)


def vmem(count):
    return [pl.BlockSpec(memory_space=pltpu.VMEM)] * count


LIMIT = pltpu.CompilerParams(vmem_limit_bytes=24 * 2**20)


def call(body, args, outs, cost, scratch=(), in_specs=None, params=LIMIT, out_specs=None):
    return pl.pallas_call(
        body,
        out_shape=outs,
        in_specs=in_specs or vmem(len(args)),
        out_specs=out_specs or vmem(len(outs)),
        scratch_shapes=scratch,
        compiler_params=params,
        cost_estimate=pl.CostEstimate(flops=cost, bytes_accessed=cost, transcendentals=0),
    )(*args)


def gathered(q, axis):
    def swap(value, apart):
        return lax.ppermute(value, axis, [(i, i ^ apart) for i in range(lax.axis_size(axis))])

    far = swap(q, 2)
    return q, swap(q, 1), far, swap(far, 1)


def rate_term(pieces, rate_blocks, pattern, first):
    cells, levels = pieces[0].shape
    return pl.pallas_call(
        functools.partial(rate_kernel, "lev"),
        in_specs=[pl.BlockSpec(memory_space=pltpu.SMEM)] + vmem(len(pieces) + 2),
        out_specs=pl.BlockSpec(memory_space=pltpu.VMEM),
        out_shape=jax.ShapeDtypeStruct((cells, levels), jnp.float32),
        scratch_shapes=[pltpu.VMEM((cells, len(pieces) * levels), jnp.bfloat16)],
        compiler_params=LIMIT,
        cost_estimate=pl.CostEstimate(
            flops=2 * cells * rate_blocks.size, bytes_accessed=2 * rate_blocks.size, transcendentals=0
        ),
    )(pattern, *pieces, rate_blocks, first)


def shifted(value, axis):
    peers = lax.axis_size(axis)
    return lax.ppermute(value, axis, [(i, i + 1) for i in range(peers - 1)])


def local(
    populations,
    rate_blocks,
    pattern,
    bracket,
    cross_section,
    emission,
    absorber,
    stream_speed,
    cross_speed,
    inflow,
):
    cells, levels = populations.shape
    strips = lax.axis_size("cell")
    bracket = bracket.reshape(1, cells)
    pattern = pattern.T
    cross = cross_section.reshape(1, levels)
    crosses = cross_section.reshape(levels // LANES, LANES)
    emission = emission.reshape(1, levels)
    absorber = absorber.reshape(1, cells)
    stream = stream_speed.reshape(1, cells)
    crossways = cross_speed.reshape(1, cells)

    field = jax.ShapeDtypeStruct((cells, levels), jnp.float32)
    rounded = jax.ShapeDtypeStruct((cells, levels), jnp.bfloat16)
    layer = jax.ShapeDtypeStruct((NY, levels), jnp.bfloat16)
    tiles = jax.ShapeDtypeStruct((strips, ROWS, LANES), jnp.float32)
    size = cells * levels * 4

    def swap(value):
        return lax.all_to_all(value, "cell", 0, 0, tiled=True)

    sources = (populations, cross, emission, absorber)
    q, last, leaving = call(
        first_kernel,
        sources,
        (rounded, layer, jax.ShapeDtypeStruct((strips, 2 * ROWS, LANES), jnp.bfloat16)),
        LONG * size,
        [pltpu.VMEM(value.shape, value.dtype) for value in sources]
        + [pltpu.SemaphoreType.DMA((len(sources) - 1 + CHUNKS,))],
        [pl.BlockSpec(memory_space=pl.ANY)] * len(sources),
        pltpu.CompilerParams(vmem_limit_bytes=FIRST * 2**20),
    )
    pieces = gathered(q, "lev")
    (first,) = call(
        first_bracket_kernel,
        (bracket,),
        (jax.ShapeDtypeStruct((cells, LANES), jnp.float32),),
        LONG * size,
    )
    last, first = lax.optimization_barrier((last, first))
    arrived = shifted(last, "cell")
    sent, rates = lax.optimization_barrier(
        (swap(leaving), rate_term(pieces, rate_blocks, pattern, first))
    )
    entered, passes = call(
        functools.partial(first_scan_kernel, "cell", cells // NY),
        (sent, crosses),
        (tiles, tiles),
        size,
        [pltpu.VMEM(tiles.shape, jnp.float32)],
    )
    same, other = call(
        functools.partial(response_kernel, "cell", cells // NY),
        (sent, crosses, emission.reshape(crosses.shape)),
        (tiles, tiles),
        size,
    )
    part, leaving = call(
        functools.partial(step_kernel, False, "cell"),
        (populations, rates, entered, arrived, inflow, cross, emission, absorber, stream, crossways),
        (field, jax.ShapeDtypeStruct((strips, 2 * ROWS, LANES), jnp.float32)),
        5 * size,
    )
    swapped = swap(leaving)
    middle, q, last = call(
        middle_kernel, (part, swapped, cross, absorber), (field, rounded, layer), 3 * size
    )
    pieces = gathered(q, "lev")
    arrived = shifted(last, "cell")
    (entering,) = call(
        second_scan_kernel,
        (swapped, entered, passes, same, other),
        (tiles,),
        size,
        [pltpu.VMEM(tiles.shape, jnp.float32)],
    )
    entering = swap(entering)
    rates = rate_term(pieces, rate_blocks, pattern, first)
    return call(
        functools.partial(step_kernel, True, "cell"),
        (middle, rates, entering, arrived, inflow, cross, emission, absorber, stream, crossways, populations),
        (field, field),
        5 * size,
        [pltpu.VMEM(field.shape, field.dtype)] * 2 + [pltpu.SemaphoreType.DMA((2, CHUNKS))],
        out_specs=[pl.BlockSpec(memory_space=pl.ANY)] * 2,
    )


def solution(mesh):
    in_specs = (
        P("cell", "lev"),
        P(None, "lev", None, None, None),
        P("lev", None),
        P("cell"),
        P("lev"),
        P("lev"),
        P("cell"),
        P("cell"),
        P("cell"),
        P(None, "lev"),
    )
    out_specs = (P("cell", "lev"), P("cell", "lev"))
    return jax.shard_map(local, mesh=mesh, in_specs=in_specs, out_specs=out_specs, check_vma=False)
```
